128 devices in a mesh: dom: 32 (over y, z, core), case: 4 (over x).
Axes of the slice: x: 4, y: 4, z: 4, core: 2. Of those that a mesh axis runs over, the one named last changes fastest.
Arguments:
- dual_ops: float32 [64, 1536, 1536], P('dom')
- modes: bfloat16 [64, 16, 1536], P('dom'), may hold values from -0.15625 to 0.15625
- coarse_rows: float32 [64, 8, 16, 16], P('dom'), may hold values from -1 to 1
- coarse_cols: int32 [64, 8], P('dom'), may hold values from 0 to 63, as said below
- row_perm: int32 [64, 1536], P('dom'), may hold values from 0 to 1535, each once within a row
- iface_size: int32 [64], P('dom'), may hold values from 256 to 768, as said below
- rhs: float32 [64, 768, 512], P('dom', None, 'case'), may hold values from -6 to 6
Outputs:
- solution: float32 [64, 768, 512], P('dom', None, 'case')
- residual: float32 [64, 768, 512], P('dom', None, 'case')
- history: float32 [4, 512], P(None, 'case')
- peak_norm: float32 [4], replicated
The draws below stay inside these ranges and needn't reach their ends.
Inputs may be any that keep to these rules, and one draw needn't show every extreme that they name: `iface_size`: interfaces carry between 256 and 768 multipliers; both ends are reached in every draw. `coarse_cols`: for every subdomain s the first three entries are s, (s - 1) mod 64 and (s + 1) mod 64; the others are any subdomains, repeats allowed. `row_perm`: each row is a permutation of the local rows.
All inputs are finite; a program needn't handle non-finite values.
Results may differ from the reference program's by a relative error of at most 0.0056.
Values may be sent and summed in bfloat16 or wider, within the bound.
No kernel may reach another device: no remote copies, remote signals or barrier semaphores. Data moves between devices by JAX's collectives and lax.ppermute only.
A program may use at most 192 MiB of HBM per device.

```python
import jax
import jax.numpy as jnp
from jax import lax

NMAX = 1536
MODES = 16
NB = 8
STEPS = 4
MMAX = 768
MMIN = 256
DOMS = 64
CASES = 512


def draw_dual_ops(key, part):

    def single(position):
        subkey = jax.random.fold_in(jax.random.fold_in(key, 17), position)
        first_key, second_key = jax.random.split(subkey, 2)
        noise = jax.random.normal(first_key, (NMAX, NMAX), jnp.float32) / jnp.sqrt(2.0 * NMAX)
        matrix = noise + noise.T
        diagonal = jax.random.uniform(second_key, (NMAX,), jnp.float32, 3.0, 5.0)
        matrix = matrix + jnp.diag(diagonal)
        return matrix
    return lax.map(single, jnp.arange(DOMS, dtype=jnp.int32))


def draw_iface_size(key, part):
    first_key, second_key, third_key, fourth_key = jax.random.split(jax.random.fold_in(key, 29), 4)
    heavy = jax.random.randint(first_key, (DOMS,), 0, 4) == 0
    higher = jax.random.randint(second_key, (DOMS,), 3 * MMAX // 4, MMAX + 1)
    lower = jax.random.randint(third_key, (DOMS,), MMIN, MMAX // 2 + 1)
    sizes = jnp.where(heavy, higher, lower)
    spots = jax.random.randint(fourth_key, (2,), 0, DOMS)
    sizes = sizes.at[spots[0]].set(MMAX)
    sizes = sizes.at[(spots[0] + 1 + spots[1] % (DOMS - 1)) % DOMS].set(MMIN)
    return sizes.astype(jnp.int32)


def draw_coarse_cols(key, part):
    owners = jnp.arange(DOMS, dtype=jnp.int32)
    extra = jax.random.randint(jax.random.fold_in(key, 41), (DOMS, NB - 3), 0, DOMS)
    columns = [owners[:, None], ((owners - 1) % DOMS)[:, None], ((owners + 1) % DOMS)[:, None], extra]
    return jnp.concatenate(columns, axis=1).astype(jnp.int32)


def block_levels(stream_key, dims, cuts, smallest, high):
    factor_of, own = 1.0, jax.random.fold_in(stream_key, 6)
    for axis_at, parts in cuts:
        heights = jnp.exp(jax.random.uniform(jax.random.fold_in(own, axis_at), (parts,), jnp.float32, smallest / len(cuts), high / len(cuts)))
        factor_of = factor_of * jnp.repeat(heights, dims[axis_at] // parts).reshape([-1 if axis == axis_at else 1 for axis in range(len(dims))])
    return factor_of


def gaussian(key, shape, deviation, reach, shards=(), kind=jnp.bfloat16):
    array = jax.random.normal(key, shape, jnp.float32) * deviation
    if len(shards) > 0:
        array = block_levels(key, shape, shards, -0.22, 0.18) * array
    return jnp.clip(array, min=-reach, max=reach).astype(kind)


def setup_inputs(seed: int = 0) -> dict:
    streams_of = jax.random.split(jax.random.key(seed), 8)
    dual_ops = draw_dual_ops(jax.random.fold_in(streams_of[7], 71), 0)
    modes = gaussian(streams_of[1], (DOMS, MODES, NMAX), NMAX ** -0.5, 0.15625, ((0, 32),))
    coarse_rows = gaussian(streams_of[2], (DOMS, NB, MODES, MODES), 0.15, 1.0, ((0, 32),), jnp.float32)
    coarse_cols = draw_coarse_cols(jax.random.fold_in(streams_of[7], 71), 0)
    row_perm = jax.vmap(lambda own: jax.random.permutation(own, NMAX))(jax.random.split(streams_of[4], DOMS)).reshape((DOMS, NMAX)).astype(jnp.int32)
    iface_size = draw_iface_size(jax.random.fold_in(streams_of[7], 71), 0)
    rhs = gaussian(streams_of[6], (DOMS, MMAX, CASES), 1.0, 6.0, ((0, 32), (2, 4)), jnp.float32)
    return dict(dual_ops=dual_ops, modes=modes, coarse_rows=coarse_rows, coarse_cols=coarse_cols, row_perm=row_perm, iface_size=iface_size, rhs=rhs)


low_bound = 2.0
high_bound = 14.0
epsilon = 1e-06
highest = lax.Precision.HIGHEST

def pick_rows(source, rows_index):
    return jax.vmap(lambda block_rows, chosen: block_rows[chosen])(source, rows_index)

def build_local(vector, inverse):
    left_side = jnp.roll(vector, 1, axis=0)
    return pick_rows(jnp.concatenate([-left_side, vector], axis=1), inverse)

def assemble(local_rows, row_perm, live_mask):
    combined = pick_rows(local_rows, row_perm)
    half_width = combined.shape[1] // 2
    return (combined[:, half_width:] - jnp.roll(combined[:, :half_width], -1, axis=0)) * live_mask

def coarse(local_rows, modes_wide, coarse_rows, coarse_cols):
    coefficients = jnp.einsum('sjn,snc->sjc', modes_wide, local_rows, precision=highest).astype(jnp.bfloat16)
    coefficients = lax.optimization_barrier(coefficients)
    picked = coefficients[coarse_cols].astype(jnp.float32)
    amounts = jnp.einsum('sqij,sqjc->sic', coarse_rows, picked, precision=highest)
    return jnp.einsum('sjn,sjc->snc', modes_wide, amounts, precision=highest)

def reference(dual_ops, modes, coarse_rows, coarse_cols, row_perm, iface_size, rhs):
    half_width = rhs.shape[1]
    live_mask = (jnp.arange(half_width, dtype=jnp.int32)[None, :] < iface_size[:, None]).astype(jnp.float32)[:, :, None]
    counter = jnp.broadcast_to(jnp.arange(row_perm.shape[1], dtype=jnp.int32)[None, :], row_perm.shape)
    inverse = jax.vmap(lambda ordering, values: jnp.zeros_like(ordering).at[ordering].set(values))(row_perm, counter)
    modes_wide = modes.astype(jnp.float32)

    def project(vector):
        local_rows = build_local(vector, inverse)
        return vector - assemble(coarse(local_rows, modes_wide, coarse_rows, coarse_cols), row_perm, live_mask)

    def operator(vector):
        local_rows = build_local(vector, inverse)
        product = jnp.einsum('snm,smc->snc', dual_ops, local_rows, precision=highest)
        return assemble(product, row_perm, live_mask)
    centre = 0.5 * (high_bound + low_bound)
    radius = 0.5 * (high_bound - low_bound)
    spread_ratio = centre / radius
    ratio_now = 1.0 / spread_ratio
    residual = project(rhs * live_mask)
    direction = residual / centre
    solution = jnp.zeros_like(rhs)
    norm_list = []
    for turn_index in range(STEPS):
        solution = solution + direction
        residual = residual - project(operator(direction))
        norm_list.append(jnp.sqrt(lax.optimization_barrier(jnp.sum(residual * residual, axis=(0, 1))) + epsilon))
        if turn_index + 1 < STEPS:
            ratio_next = 1.0 / (2.0 * spread_ratio - ratio_now)
            direction = ratio_next * ratio_now * direction + 2.0 * ratio_next / radius * residual
            ratio_now = ratio_next
    history = jnp.stack(norm_list)
    return (solution, residual, history, lax.optimization_barrier(jnp.max(history, axis=1)))
```

```python
import jax
import jax.numpy as jnp
from jax import lax
from jax.experimental import pallas as pl
from jax.experimental.pallas import tpu as pltpu
from jax.sharding import PartitionSpec as P

STEPS = 4

low_bound = 2.0
high_bound = 14.0
epsilon = 1e-06
f32 = jnp.float32
bf16 = jnp.bfloat16
BLK = 256
VMEM = pl.BlockSpec(memory_space=pltpu.VMEM)
SMEM = pl.BlockSpec(memory_space=pltpu.SMEM)
ANY = pl.BlockSpec(memory_space=pl.ANY)
PARAMS = pltpu.CompilerParams(vmem_limit_bytes=40 * 1024 * 1024)


def from_behind(block, axis, distance):
    count = lax.axis_size(axis)
    route = [((i - distance) % count, i) for i in range(count)]
    return lax.ppermute(block, axis, route)


def dot(a, b):
    return jnp.dot(a, b, preferred_element_type=f32)


def split(value):
    high = value.astype(bf16)
    low = (value - high.astype(f32)).astype(bf16)
    return high, low


def slot_modes_kernel(modes_ref, perm_ref, left_ref, right_ref, to_next_ref, to_prior_ref):
    count, rows, width = modes_ref.shape
    half = width // 2
    for s in range(count):
        for at in range(0, width, BLK):
            one_hot = (
                lax.broadcasted_iota(jnp.int32, (width, BLK), 0) == perm_ref[s : s + 1, at : at + BLK]
            ).astype(f32).astype(bf16)
            part = dot(modes_ref[s], one_hot).astype(bf16)
            if at < half:
                left_ref[s, :, at : at + BLK] = part
                if s == 0:
                    to_prior_ref[:, at : at + BLK] = part
            else:
                right_ref[s, :, at - half : at - half + BLK] = part
                if s == count - 1:
                    to_next_ref[:, at - half : at - half + BLK] = part


def slot_modes(modes, row_perm):
    count, rows, width = modes.shape
    half = width // 2
    side = jax.ShapeDtypeStruct((count, rows, half), bf16)
    rim = jax.ShapeDtypeStruct((rows, half), bf16)
    return pl.pallas_call(
        slot_modes_kernel,
        out_shape=(side, side, rim, rim),
        in_specs=[VMEM, VMEM],
        out_specs=[VMEM] * 4,
        compiler_params=PARAMS,
        name="slot_modes",
    )(modes, row_perm)


def slot_op_kernel(ops_ref, perm_ref, out_ref, diag_ref, cols_done, one_hot, diag_row):
    width = one_hot.shape[0]
    blocks = width // BLK
    at = pl.program_id(0)

    @pl.when(at == 0)
    def _():
        for k in range(blocks):
            one_hot[k * BLK : (k + 1) * BLK, :] = (
                lax.broadcasted_iota(jnp.int32, (BLK, width), 0) + k * BLK == perm_ref[...]
            ).astype(f32).astype(bf16)
        diag_row[...] = jnp.zeros_like(diag_row)

    @pl.when(at < blocks)
    def _():
        block = ops_ref[0]
        on_diag = lax.broadcasted_iota(jnp.int32, (BLK, width), 0) + at * BLK == (
            lax.broadcasted_iota(jnp.int32, (BLK, width), 1)
        )
        diag_row[0:1, :] += jnp.sum(jnp.where(on_diag, block, 0.0), axis=0, keepdims=True)
        rest = jnp.where(on_diag, 0.0, block).astype(bf16)
        rows = pl.ds(pl.multiple_of(at * BLK, BLK), BLK)
        cols_done[rows, :] = dot(rest, one_hot[...]).astype(bf16)

    @pl.when(at >= blocks)
    def _():
        place = pl.multiple_of((at - blocks) * BLK, BLK)
        perm_part = perm_ref[:, pl.ds(place, BLK)].astype(f32)
        owner = jnp.transpose(jnp.broadcast_to(perm_part, (128, BLK)))
        total = jnp.zeros((BLK, 128), f32)
        pieces = []
        for k in range(0, width, 128):
            here = (lax.broadcasted_iota(jnp.int32, (BLK, 128), 1) + k).astype(f32) == owner
            pieces.append(here.astype(f32).astype(bf16))
            total += jnp.where(here, diag_row[0:1, k : k + 128], 0.0)
        out_ref[...] = dot(jnp.concatenate(pieces, axis=1), cols_done[...]).astype(bf16)
        diag_ref[...] = jnp.broadcast_to(jnp.sum(total, axis=1, keepdims=True), (BLK, 128))


def slot_op(dual_ops, perm_row, which):
    width = dual_ops.shape[1]
    blocks = width // BLK
    return pl.pallas_call(
        slot_op_kernel,
        grid=(2 * blocks,),
        out_shape=(
            jax.ShapeDtypeStruct((width, width), bf16),
            jax.ShapeDtypeStruct((width, 128), f32),
        ),
        in_specs=[
            pl.BlockSpec((1, BLK, width), lambda i: (which, jnp.minimum(i, blocks - 1), 0)),
            pl.BlockSpec((1, width), lambda i: (0, 0)),
        ],
        out_specs=[
            pl.BlockSpec((BLK, width), lambda i: (jnp.maximum(i - blocks, 0), 0)),
            pl.BlockSpec((BLK, 128), lambda i: (jnp.maximum(i - blocks, 0), 0)),
        ],
        scratch_shapes=[
            pltpu.VMEM((width, width), bf16),
            pltpu.VMEM((width, width), bf16),
            pltpu.VMEM((8, width), f32),
        ],
        compiler_params=PARAMS,
        cost_estimate=pl.CostEstimate(
            flops=4 * width**3, bytes_accessed=6 * width * width, transcendentals=0
        ),
        name="slot_op",
    )(dual_ops, perm_row)


def alive(size, rows):
    return lax.broadcasted_iota(jnp.int32, (rows, 128), 0) < size


def partial_coefficients(rows_ref, shares, part_ref):
    modes = part_ref.shape[1]
    sums = []
    for e, share in enumerate(shares):
        if share is None:
            sums.append(jnp.zeros((2 * modes, 128), f32))
            continue
        high, low = split(share)
        both = dot(rows_ref[e], jnp.concatenate([high, low], axis=1))
        sums.append(both[:, :128] + both[:, 128:])
    part_ref[0] = sums[0][:modes]
    part_ref[1] = sums[0][modes:] + sums[1][:modes]
    part_ref[2] = sums[1][modes:] + sums[2][:modes]
    part_ref[3] = sums[2][modes:]


def start_kernel(
    sizes_ref, left_ref, right_ref, prior_ref, next_ref, rhs_ref, rows_ref, cols_ref, part_ref
):
    half = rhs_ref.shape[1]
    pairs = [
        (prior_ref[...], left_ref[0]),
        (right_ref[0], left_ref[1]),
        (right_ref[1], next_ref[...]),
    ]
    for e, (above, below) in enumerate(pairs):
        stack = jnp.concatenate([above.astype(f32), -below.astype(f32)], axis=0)
        rows_ref[e] = stack.astype(bf16)
        cols_ref[e] = jnp.transpose(jnp.concatenate([stack, stack], axis=0)).astype(bf16)
    shares = [None]
    for e in range(2):
        shares.append(jnp.where(alive(sizes_ref[e + 1], half), -rhs_ref[e], 0.0))
    partial_coefficients(rows_ref, shares, part_ref)


def start(sizes, left, right, prior, following, rhs):
    half = rhs.shape[1]
    modes = left.shape[1]
    return pl.pallas_call(
        start_kernel,
        out_shape=(
            jax.ShapeDtypeStruct((3, 2 * modes, half), bf16),
            jax.ShapeDtypeStruct((3, half, 4 * modes), bf16),
            jax.ShapeDtypeStruct((4, modes, 128), f32),
        ),
        in_specs=[SMEM] + [VMEM] * 5,
        out_specs=[VMEM] * 3,
        compiler_params=PARAMS,
        name="start",
    )(sizes, left, right, prior, following, rhs)


def step_kernel(first, last, old, new, *refs):
    refs = list(refs)
    take = lambda n: [refs.pop(0) for _ in range(n)]
    sizes_ref, own_ref, other_ref = take(3)
    all_ref, blocks_ref, rows_ref, cols_ref = take(4)
    if first:
        rhs_ref, from_prior_ref = take(2)
    else:
        wa_ref, wb_ref, wc_ref, from_prior_ref, from_next_ref, res_ref = take(6)
    if not last:
        if not first:
            dir_ref, sol_ref = take(2)
        op_refs = take(2)
        diag_refs = take(2)
    res_out, norm_out = take(2)
    if not last:
        dir_out, sol_out, wa_out, wb_out, wc_out, part_out = take(6)
    picked = take(1)[0]
    if not last:
        held, slots, sems = take(3)
        copies = []
        for s in range(2):
            copies.append(pltpu.make_async_copy(op_refs[s], held.at[s], sems.at[s]))
            copies[-1].start()
    half = res_out.shape[1]
    modes = all_ref.shape[1]
    subs, _, width = blocks_ref.shape
    count = width // modes
    amounts = []
    for s in range(subs):
        for q in range(count):
            value = all_ref[own_ref[s * count + q]] + all_ref[other_ref[s * count + q]]
            picked[s, q * modes : (q + 1) * modes, :] = value.astype(bf16)
        high, low = split(blocks_ref[s])
        both = dot(jnp.concatenate([high, low], axis=0), picked[s])
        amounts.append(both[:modes] + both[modes:])
    total = jnp.zeros((1, 128), f32)
    live = [alive(sizes_ref[e], half) for e in range(3)]
    for e in range(3):
        high, low = split(jnp.concatenate([amounts[e], amounts[e + 1]], axis=0))
        spread = dot(cols_ref[e], jnp.concatenate([high, low], axis=0))
        if first:
            field = -from_prior_ref[...] if e == 0 else -rhs_ref[e - 1]
            residual = jnp.where(live[e], spread - field, 0.0)
        else:
            field = (wa_ref, wb_ref, wc_ref)[e][...]
            if e == 0:
                field = field + from_prior_ref[...]
            if e == 2:
                field = field + from_next_ref[...]
            residual = res_ref[e] + (jnp.where(live[e], spread, 0.0) - field)
        if last:
            if e > 0:
                res_out[e - 1] = residual
        else:
            res_out[e] = residual
        if e > 0:
            total += jnp.sum(residual * residual, axis=0, keepdims=True)
        if not last:
            direction = new * residual
            if not first:
                direction = direction + old * dir_ref[e]
            dir_out[e] = direction
            if e > 0:
                sol_out[e - 1] = direction if first else sol_ref[e - 1] + direction
            low_form = direction.astype(bf16)
            if e < 2:
                slots[e, :half] = -low_form
            if e > 0:
                slots[e - 1, half:] = low_form
    norm_out[...] = total
    if last:
        return
    sides = []
    for s in range(2):
        copies[s].wait()
        left_at, right_at = s, s + 1
        for side, (e, sign) in enumerate(((left_at, -1.0), (right_at, 1.0))):
            parts = []
            for at in range(0, half, BLK):
                here = slice(side * half + at, side * half + at + BLK)
                exact = diag_refs[s][here, :] * dir_out[e, at : at + BLK, :]
                parts.append(dot(held[s, here, :], slots[s]) + sign * exact)
            sides.append(jnp.concatenate(parts, axis=0))
    shares = [
        jnp.where(live[0], -sides[0], 0.0),
        jnp.where(live[1], sides[1] - sides[2], 0.0),
        jnp.where(live[2], sides[3], 0.0),
    ]
    wa_out[...], wb_out[...], wc_out[...] = shares
    partial_coefficients(rows_ref, shares, part_out)


def step(first, last, old, new, ints, constants, fields, ops=()):
    half, lanes = fields[-1].shape[-2:]
    modes = constants[0].shape[1]
    field = jax.ShapeDtypeStruct((half, lanes), f32)
    three = jax.ShapeDtypeStruct((3, half, lanes), f32)
    two = jax.ShapeDtypeStruct((2, half, lanes), f32)
    norm = jax.ShapeDtypeStruct((1, lanes), f32)
    subs, _, width = constants[1].shape
    out = [two if last else three, norm]
    scratch = [pltpu.VMEM((subs, width, lanes), bf16)]
    specs = [SMEM] * len(ints) + [VMEM] * (len(constants) + len(fields))
    if not last:
        part = jax.ShapeDtypeStruct((4, modes, lanes), f32)
        out += [three, two, field, field, field, part]
        scratch += [
            pltpu.VMEM((2, 2 * half, 2 * half), bf16),
            pltpu.VMEM((2, 2 * half, lanes), bf16),
            pltpu.SemaphoreType.DMA((2,)),
        ]
        specs += [ANY, ANY, VMEM, VMEM]

    def body(*refs):
        step_kernel(first, last, old, new, *refs)

    return pl.pallas_call(
        body,
        out_shape=tuple(out),
        in_specs=specs,
        out_specs=[VMEM] * len(out),
        scratch_shapes=scratch,
        compiler_params=PARAMS,
        cost_estimate=pl.CostEstimate(
            flops=10**9, bytes_accessed=15 * 10**6, transcendentals=0
        ),
        name="last_step" if last else "step",
    )(*ints, *constants, *fields, *ops)


def to_everyone(value, axis):
    size = lax.psum(1, axis)
    return lax.all_to_all(
        jnp.broadcast_to(value[None], (size, *value.shape)), axis, 0, 0, tiled=True
    )


def shards(dual_ops, modes, coarse_rows, coarse_cols, row_perm, iface_size, rhs):
    doms = lax.axis_size("dom")
    count, blocks, rows, _ = coarse_rows.shape
    flat = jnp.swapaxes(coarse_rows, 1, 2).reshape(count, rows, blocks * rows)
    whole = jnp.concatenate([coarse_cols, iface_size[:, None]], axis=1).astype(f32)
    whole = jnp.pad(whole, ((0, 0), (0, blocks * rows - whole.shape[1])))
    pack = jnp.concatenate([flat, jnp.broadcast_to(whole[:, None], (count, 8, blocks * rows))], axis=1)
    prior_pack = from_behind(pack[-1], "dom", 1)
    next_pack = from_behind(pack[0], "dom", -1)
    prior_rhs = from_behind(rhs[-1], "dom", 1)
    left, right, to_next, to_prior = slot_modes(modes, row_perm)
    prior_modes = from_behind(to_next, "dom", 1)
    next_modes = from_behind(to_prior, "dom", -1)
    ext = jnp.concatenate([prior_pack[None], pack, next_pack[None]], axis=0)
    ext_blocks = ext[:, :rows]
    ext_whole = ext[:, rows].astype(jnp.int32)
    cols = ext_whole[:, :blocks].reshape(-1)
    sizes = ext_whole[:3, blocks]
    odd = cols % 2
    own = 4 * (cols // 2) + 1 + odd
    other = (own + 4 * odd - 2) % (4 * doms)
    ints = (sizes, own, other)

    ops_a, diag_a = slot_op(dual_ops, row_perm[0:1], 0)
    row_forms, col_forms, part = start(sizes, left, right, prior_modes, next_modes, rhs)
    second_perm, _ = lax.optimization_barrier((row_perm[1:2], part))
    everything = to_everyone(part, "dom").reshape(4 * doms, rows, -1)
    ops_b, diag_b = slot_op(dual_ops, second_perm, 1)
    ops = (ops_a, ops_b, diag_a, diag_b)

    centre = 0.5 * (high_bound + low_bound)
    radius = 0.5 * (high_bound - low_bound)
    spread_ratio = centre / radius
    ratio_now = 1.0 / spread_ratio
    norms = []
    old, new = 0.0, 1.0 / centre
    constants = (everything, ext_blocks, row_forms, col_forms)
    residual, _, direction, solution, wa, wb, wc, part = step(
        True, False, old, new, ints, constants, (rhs, prior_rhs), ops
    )
    for turn in range(STEPS):
        from_prior = from_behind(wc, "dom", 1)
        from_next = from_behind(wa, "dom", -1)
        everything = to_everyone(part, "dom").reshape(4 * doms, rows, -1)
        constants = (everything, ext_blocks, row_forms, col_forms)
        fields = (wa, wb, wc, from_prior, from_next, residual)
        if turn + 1 < STEPS:
            ratio_next = 1.0 / (2.0 * spread_ratio - ratio_now)
            old, new = ratio_next * ratio_now, 2.0 * ratio_next / radius
            ratio_now = ratio_next
            residual, norm, direction, solution, wa, wb, wc, part = step(
                False, False, old, new, ints, constants, fields + (direction, solution), ops
            )
        else:
            residual, norm = step(False, True, 0.0, 0.0, ints, constants, fields)
        norms.append(norm)
    sums = to_everyone(jnp.concatenate(norms, axis=0), ("dom", "case"))
    cases = lax.axis_size("case")
    totals = jnp.sum(sums.reshape(doms, cases, STEPS, -1), axis=0)
    whole_history = jnp.sqrt(totals + epsilon)
    history = lax.dynamic_index_in_dim(whole_history, lax.axis_index("case"), 0, keepdims=False)
    peak_norm = jnp.max(whole_history, axis=(0, 2))
    return (solution, residual, history, peak_norm)


def solution(mesh):
    in_specs = (
        P("dom", None, None),
        P("dom", None, None),
        P("dom", None, None, None),
        P("dom", None),
        P("dom", None),
        P("dom"),
        P("dom", None, "case"),
    )
    out_specs = (P("dom", None, "case"), P("dom", None, "case"), P(None, "case"), P())
    return jax.shard_map(shards, mesh=mesh, in_specs=in_specs, out_specs=out_specs, check_vma=False)
```

```python
import jax
import jax.numpy as jnp
from jax import lax
from jax.experimental import pallas as pl
from jax.experimental.pallas import tpu as pltpu
from jax.sharding import PartitionSpec as P

STEPS = 4

low_bound = 2.0
high_bound = 14.0
epsilon = 1e-06
f32 = jnp.float32
bf16 = jnp.bfloat16
BLK = 256
OPBLK = 512
VECBLK = 768
VMEM = pl.BlockSpec(memory_space=pltpu.VMEM)
SMEM = pl.BlockSpec(memory_space=pltpu.SMEM)
ANY = pl.BlockSpec(memory_space=pl.ANY)
PARAMS = pltpu.CompilerParams(vmem_limit_bytes=60 * 1024 * 1024)


def from_behind(block, axis, distance):
    count = lax.axis_size(axis)
    route = [((i - distance) % count, i) for i in range(count)]
    return lax.ppermute(block, axis, route)


def dot(a, b):
    return jnp.dot(a, b, preferred_element_type=f32)


def split(value):
    high = value.astype(bf16)
    low = (value - high.astype(f32)).astype(bf16)
    return high, low


def slot_modes_kernel(modes_ref, perm_ref, left_ref, right_ref, to_next_ref, to_prior_ref):
    count, rows, width = modes_ref.shape
    half = width // 2
    for s in range(count):
        for at in range(0, width, BLK):
            one_hot = (
                lax.broadcasted_iota(jnp.int32, (width, BLK), 0) == perm_ref[s : s + 1, at : at + BLK]
            ).astype(f32).astype(bf16)
            part = dot(modes_ref[s], one_hot).astype(bf16)
            if at < half:
                left_ref[s, :, at : at + BLK] = part
                if s == 0:
                    to_prior_ref[:, at : at + BLK] = part
            else:
                right_ref[s, :, at - half : at - half + BLK] = part
                if s == count - 1:
                    to_next_ref[:, at - half : at - half + BLK] = part


def slot_modes(modes, row_perm):
    count, rows, width = modes.shape
    half = width // 2
    side = jax.ShapeDtypeStruct((count, rows, half), bf16)
    rim = jax.ShapeDtypeStruct((rows, half), bf16)
    return pl.pallas_call(
        slot_modes_kernel,
        out_shape=(side, side, rim, rim),
        in_specs=[VMEM, VMEM],
        out_specs=[VMEM] * 4,
        compiler_params=PARAMS,
        name="slot_modes",
    )(modes, row_perm)


def slot_op_kernel(ops_ref, perm_ref, out_ref, diag_ref, cols_done, one_hot, diag_row):
    width = one_hot.shape[0]
    blocks = width // OPBLK
    at = pl.program_id(0)

    @pl.when(at == 0)
    def _():
        for k in range(blocks):
            one_hot[k * OPBLK : (k + 1) * OPBLK, :] = (
                lax.broadcasted_iota(jnp.int32, (OPBLK, width), 0) + k * OPBLK == perm_ref[...]
            ).astype(f32).astype(bf16)
        diag_row[...] = jnp.zeros_like(diag_row)

    @pl.when(at < blocks)
    def _():
        block = ops_ref[0]
        on_diag = lax.broadcasted_iota(jnp.int32, (OPBLK, width), 0) + at * OPBLK == (
            lax.broadcasted_iota(jnp.int32, (OPBLK, width), 1)
        )
        diag_row[0:1, :] += jnp.sum(jnp.where(on_diag, block, 0.0), axis=0, keepdims=True)
        rest = jnp.where(on_diag, 0.0, block).astype(bf16)
        rows = pl.ds(pl.multiple_of(at * OPBLK, OPBLK), OPBLK)
        cols_done[rows, :] = dot(rest, one_hot[...]).astype(bf16)

    @pl.when(at >= blocks)
    def _():
        place = pl.multiple_of((at - blocks) * OPBLK, OPBLK)
        perm_part = perm_ref[:, pl.ds(place, OPBLK)].astype(f32)
        owner = jnp.transpose(jnp.broadcast_to(perm_part, (128, OPBLK)))
        total = jnp.zeros((OPBLK, 128), f32)
        pieces = []
        for k in range(0, width, 128):
            here = (lax.broadcasted_iota(jnp.int32, (OPBLK, 128), 1) + k).astype(f32) == owner
            pieces.append(here.astype(f32).astype(bf16))
            total += jnp.where(here, diag_row[0:1, k : k + 128], 0.0)
        out_ref[...] = dot(jnp.concatenate(pieces, axis=1), cols_done[...]).astype(bf16)
        diag_ref[...] = jnp.broadcast_to(jnp.sum(total, axis=1, keepdims=True), (OPBLK, 128))


def slot_op(dual_ops, perm_row, which):
    width = dual_ops.shape[1]
    blocks = width // OPBLK
    return pl.pallas_call(
        slot_op_kernel,
        grid=(2 * blocks,),
        out_shape=(
            jax.ShapeDtypeStruct((width, width), bf16),
            jax.ShapeDtypeStruct((width, 128), f32),
        ),
        in_specs=[
            pl.BlockSpec((1, OPBLK, width), lambda i: (which, jnp.minimum(i, blocks - 1), 0)),
            pl.BlockSpec((1, width), lambda i: (0, 0)),
        ],
        out_specs=[
            pl.BlockSpec((OPBLK, width), lambda i: (jnp.maximum(i - blocks, 0), 0)),
            pl.BlockSpec((OPBLK, 128), lambda i: (jnp.maximum(i - blocks, 0), 0)),
        ],
        scratch_shapes=[
            pltpu.VMEM((width, width), bf16),
            pltpu.VMEM((width, width), bf16),
            pltpu.VMEM((8, width), f32),
        ],
        compiler_params=PARAMS,
        cost_estimate=pl.CostEstimate(
            flops=4 * width**3, bytes_accessed=6 * width * width, transcendentals=0
        ),
        name="slot_op",
    )(dual_ops, perm_row)


def alive(size, rows):
    return lax.broadcasted_iota(jnp.int32, (rows, 128), 0) < size


def partial_coefficients(rows_ref, shares, part_ref):
    modes = part_ref.shape[2]
    sums = []
    for e, share in enumerate(shares):
        if share is None:
            sums.append(jnp.zeros((2 * modes, 128), f32))
            continue
        high, low = split(share)
        both = dot(rows_ref[e], jnp.concatenate([high, low], axis=1))
        sums.append(both[:, :128] + both[:, 128:])
    parts = [
        sums[0][:modes],
        sums[0][modes:] + sums[1][:modes],
        sums[1][modes:] + sums[2][:modes],
        sums[2][modes:],
    ]
    for k, part in enumerate(parts):
        part = part.astype(bf16)
        for device in range(part_ref.shape[0]):
            part_ref[device, k] = part


def start_kernel(
    sizes_ref, left_ref, right_ref, prior_ref, next_ref, rhs_ref, rows_ref, cols_ref, part_ref
):
    half = rhs_ref.shape[1]
    pairs = [
        (prior_ref[...], left_ref[0]),
        (right_ref[0], left_ref[1]),
        (right_ref[1], next_ref[...]),
    ]
    for e, (above, below) in enumerate(pairs):
        stack = jnp.concatenate([above.astype(f32), -below.astype(f32)], axis=0)
        rows_ref[e] = stack.astype(bf16)
        cols_ref[e] = jnp.transpose(jnp.concatenate([stack, stack], axis=0)).astype(bf16)
    shares = [None]
    for e in range(2):
        shares.append(jnp.where(alive(sizes_ref[e + 1], half), -rhs_ref[e], 0.0))
    partial_coefficients(rows_ref, shares, part_ref)


def start(sizes, left, right, prior, following, rhs):
    half = rhs.shape[1]
    modes = left.shape[1]
    return pl.pallas_call(
        start_kernel,
        out_shape=(
            jax.ShapeDtypeStruct((3, 2 * modes, half), bf16),
            jax.ShapeDtypeStruct((3, half, 4 * modes), bf16),
            jax.ShapeDtypeStruct((lax.axis_size("dom"), 4, modes, 128), bf16),
        ),
        in_specs=[SMEM] + [VMEM] * 5,
        out_specs=[VMEM] * 3,
        compiler_params=PARAMS,
        name="start",
    )(sizes, left, right, prior, following, rhs)


def triple(value):
    high, low = split(value)
    return jnp.concatenate([high, low, high, jnp.zeros_like(high)], axis=1)


def triple_rows(value):
    high, low = split(value)
    return jnp.concatenate([high, high, low, jnp.zeros_like(high)], axis=0)


def share_sums(rows_ref, shares):
    modes = rows_ref.shape[1] // 2
    sums = []
    for e, share in enumerate(shares):
        lanes = share.shape[1]
        high, low = split(share)
        both = dot(rows_ref[e], jnp.concatenate([high, low], axis=1))
        sums.append(both[:, :lanes] + both[:, lanes:])
    return jnp.concatenate(
        [
            sums[0][:modes],
            sums[0][modes:] + sums[1][:modes],
            sums[1][modes:] + sums[2][:modes],
            sums[2][modes:],
        ],
        axis=0,
    )


def own_shares(live, sides):
    return [
        jnp.where(live[0], -sides[0], 0.0),
        jnp.where(live[1], sides[1] - sides[2], 0.0),
        jnp.where(live[2], sides[3], 0.0),
    ]


def apply_operator(copies, held, slots, diag_refs, exact):
    sides = []
    half = exact(0).shape[0]
    for s in range(2):
        copies[s].wait()
        for side in range(2):
            here = slice(side * half, side * half + half)
            value = dot(held[s, here, :], slots[s])
            sign = 1.0 if side else -1.0
            lanes = exact(s + side).shape[1]
            diag = diag_refs[s][here, :]
            if lanes > 128:
                diag = jnp.concatenate([diag, diag], axis=1)
            sides.append(value + sign * (diag * exact(s + side)))
    return sides


def take_amounts(own_ref, other_ref, all_ref, blocks_ref, picked):
    modes = all_ref.shape[1]
    subs, _, width = blocks_ref.shape
    count = width // modes
    amounts = []
    for s in range(subs):
        for q in range(count):
            here = q * modes
            picked[s, here : here + modes, :] = all_ref[own_ref[s * count + q]]
            picked[s, width + here : width + here + modes, :] = all_ref[other_ref[s * count + q]]
        high, low = split(blocks_ref[s])
        rows = jnp.concatenate([high, low], axis=0)
        both = dot(jnp.concatenate([rows, rows], axis=1), picked[s])
        amounts.append(both[:modes] + both[modes:])
    return jnp.concatenate(amounts, axis=0)


def first_kernel(
    scale, sizes_ref, rhs_ref, prior_ref, rows_ref, cols_ref, op_a, op_b, diag_a, diag_b,
    res_out, dir_out, wa_out, wb_out, wc_out, sums_out, fields_out, links_out,
    held, slots, wide, sems,
):
    copies = []
    for s, op in enumerate((op_a, op_b)):
        copies.append(pltpu.make_async_copy(op, held.at[s], sems.at[s]))
        copies[-1].start()
    half = rhs_ref.shape[1]
    modes = rows_ref.shape[1] // 2
    live = [alive(sizes_ref[e], half) for e in range(3)]
    for e in range(3):
        start = jnp.where(live[e], prior_ref[...] if e == 0 else rhs_ref[e - 1], 0.0)
        direction = scale * start
        res_out[e] = start
        dir_out[e] = direction
        pair = cols_ref[e][:, : 2 * modes].astype(f32)
        parts = [pair, jnp.zeros((half, 128 - 2 * modes), f32)]
        if e > 0:
            parts = [jnp.zeros((half, e * modes), f32), pair]
            parts.append(jnp.zeros((half, 128 - (2 + e) * modes), f32))
        coarse = jnp.where(live[e], jnp.concatenate(parts, axis=1), 0.0)
        both = jnp.concatenate([direction, coarse], axis=1)
        wide[e] = both
        low_form = both.astype(bf16)
        if e < 2:
            slots[e, :half] = -low_form
        if e > 0:
            slots[e - 1, half:] = low_form
    sides = apply_operator(copies, held, slots, (diag_a, diag_b), lambda e: wide[e])
    live = [jnp.concatenate([mask, mask], axis=1) for mask in live]
    shares = own_shares(live, sides)
    wa_out[...], wb_out[...], wc_out[...] = [share[:, :128] for share in shares]
    sums = share_sums(rows_ref, shares)
    sums_out[...] = sums[:, :128]
    for e in range(3):
        fields_out[e] = triple(shares[e][:, 128 : 128 + 4 * modes])
    links_out[...] = triple(sums[:, 128 : 128 + 4 * modes])


def scratch_of(half, lanes):
    return [
        pltpu.VMEM((2, 2 * half, 2 * half), bf16),
        pltpu.VMEM((2, 2 * half, lanes), bf16),
    ]


def first(scale, sizes, rhs, prior_rhs, rows, cols, ops):
    half, lanes = rhs.shape[1:]
    modes = rows.shape[1] // 2
    field = jax.ShapeDtypeStruct((half, lanes), f32)
    three = jax.ShapeDtypeStruct((3, half, lanes), f32)

    def body(*refs):
        first_kernel(scale, *refs)

    return pl.pallas_call(
        body,
        out_shape=(
            three,
            three,
            field,
            field,
            field,
            jax.ShapeDtypeStruct((4 * modes, lanes), f32),
            jax.ShapeDtypeStruct((3, half, 16 * modes), bf16),
            jax.ShapeDtypeStruct((4 * modes, 16 * modes), bf16),
        ),
        in_specs=[SMEM] + [VMEM] * 4 + [ANY, ANY, VMEM, VMEM],
        out_specs=[VMEM] * 8,
        scratch_shapes=scratch_of(half, 2 * lanes)
        + [pltpu.VMEM((3, half, 2 * lanes), f32), pltpu.SemaphoreType.DMA((2,))],
        compiler_params=PARAMS,
        cost_estimate=pl.CostEstimate(
            flops=2 * 10**9, bytes_accessed=2 * 10**7, transcendentals=0
        ),
        name="first",
    )(sizes, rhs, prior_rhs, rows, cols, *ops)


def coarse_kernel(
    new, own_ref, other_ref, all_ref, blocks_ref, wa_ref, wc_ref, fields_ref,
    amounts_out, wa_out, wc_out, to_prior_out, to_next_out, picked,
):
    amounts = take_amounts(own_ref, other_ref, all_ref, blocks_ref, picked)
    amounts_out[...] = amounts
    scaled = triple_rows(new * amounts)
    wa = wa_ref[...] + dot(fields_ref[0], scaled)
    wc = wc_ref[...] + dot(fields_ref[2], scaled)
    wa_out[...], wc_out[...] = wa, wc
    to_prior_out[...], to_next_out[...] = wa.astype(bf16), wc.astype(bf16)


def share_kernel(new, amounts_ref, sums_ref, links_ref, part_out):
    modes = part_out.shape[2]
    scaled = triple_rows(new * amounts_ref[...])
    sums = (sums_ref[...] + dot(links_ref[...], scaled)).astype(bf16)
    for k in range(4):
        for device in range(part_out.shape[0]):
            part_out[device, k] = sums[k * modes : (k + 1) * modes]


def share(new, amounts, sums, links):
    rows, lanes = amounts.shape

    def body(*refs):
        share_kernel(new, *refs)

    return pl.pallas_call(
        body,
        out_shape=jax.ShapeDtypeStruct((lax.axis_size("dom"), 4, rows // 4, lanes), bf16),
        in_specs=[VMEM] * 3,
        out_specs=VMEM,
        compiler_params=PARAMS,
        cost_estimate=pl.CostEstimate(
            flops=10**11, bytes_accessed=10**9, transcendentals=0
        ),
        name="share",
    )(amounts, sums, links)


def coarse(new, ints, everything, blocks, wa, wc, fields):
    modes = everything.shape[1]
    half, lanes = wa.shape
    subs, _, width = blocks.shape
    field = jax.ShapeDtypeStruct((half, lanes), f32)
    rim = jax.ShapeDtypeStruct((half, lanes), bf16)

    def body(*refs):
        coarse_kernel(new, *refs)

    return pl.pallas_call(
        body,
        out_shape=(
            jax.ShapeDtypeStruct((4 * modes, lanes), f32),
            field,
            field,
            rim,
            rim,
        ),
        in_specs=[SMEM, SMEM] + [VMEM] * 5,
        out_specs=[VMEM] * 5,
        scratch_shapes=[pltpu.VMEM((subs, 2 * width, lanes), bf16)],
        compiler_params=PARAMS,
        cost_estimate=pl.CostEstimate(
            flops=10**8, bytes_accessed=4 * 10**6, transcendentals=0
        ),
        name="coarse",
    )(*ints, everything, blocks, wa, wc, fields)


def step_kernel(begin, last, new, old_next, new_next, *refs):
    refs = list(refs)
    take = lambda n: [refs.pop(0) for _ in range(n)]
    (sizes_ref, amounts_ref, cols_ref, fields_ref) = take(4)
    wa_ref, wb_ref, wc_ref, prior_ref, next_ref, res_ref, dir_ref = take(7)
    sol_ref = None if begin else take(1)[0]
    if not last:
        rows_ref, op_a, op_b, diag_a, diag_b = take(5)
    res_out, sol_out, norm_out = take(3)
    if not last:
        dir_out, wa_out, wb_out, wc_out, sums_out = take(5)
        held, slots, sems = take(3)
        copies = []
        for s, op in enumerate((op_a, op_b)):
            copies.append(pltpu.make_async_copy(op, held.at[s], sems.at[s]))
            copies[-1].start()
    half = wa_ref.shape[0]
    modes = amounts_ref.shape[0] // 4
    amounts = amounts_ref[...]
    high, low = split(amounts)
    live = [alive(sizes_ref[e], half) for e in range(3)]
    total = jnp.zeros((1, 128), f32)
    for e in range(3):
        if last and e == 0:
            continue
        at = slice(e * modes, (e + 2) * modes)
        spread = dot(cols_ref[e], jnp.concatenate([high[at], low[at]], axis=0))
        spread = jnp.where(live[e], spread, 0.0)
        if e == 0:
            field = wa_ref[...] + prior_ref[...].astype(f32)
        elif e == 1:
            field = wb_ref[...] + dot(fields_ref[1], triple_rows(new * amounts))
        else:
            field = wc_ref[...] + next_ref[...].astype(f32)
        residual = res_ref[e] + spread
        direction = dir_ref[e] + new * spread
        if e > 0:
            total += jnp.sum(residual * residual, axis=0, keepdims=True)
            sol_out[e - 1] = direction if begin else sol_ref[e - 1] + direction
        residual = residual - field
        if last:
            res_out[e - 1] = residual
            continue
        res_out[e] = residual
        direction = old_next * direction + new_next * residual
        dir_out[e] = direction
        low_form = direction.astype(bf16)
        if e < 2:
            slots[e, :half] = -low_form
        if e > 0:
            slots[e - 1, half:] = low_form
    norm_out[...] = total
    if last:
        return
    sides = apply_operator(copies, held, slots, (diag_a, diag_b), lambda e: dir_out[e])
    shares = own_shares(live, sides)
    wa_out[...], wb_out[...], wc_out[...] = shares
    sums_out[...] = share_sums(rows_ref, shares)


def step(begin, last, factors, sizes, amounts, cols, coarse_fields, fields, rows=None, ops=()):
    half, lanes = fields[0].shape
    field = jax.ShapeDtypeStruct((half, lanes), f32)
    three = jax.ShapeDtypeStruct((3, half, lanes), f32)
    two = jax.ShapeDtypeStruct((2, half, lanes), f32)
    out = [two if last else three, two, jax.ShapeDtypeStruct((1, lanes), f32)]
    args = [sizes, amounts, cols, coarse_fields, *fields]
    specs = [SMEM] + [VMEM] * (len(args) - 1)
    scratch = []
    if not last:
        out += [three, field, field, field, jax.ShapeDtypeStruct(amounts.shape, f32)]
        scratch += scratch_of(half, lanes) + [pltpu.SemaphoreType.DMA((2,))]
        args += [rows, *ops]
        specs += [VMEM, ANY, ANY, VMEM, VMEM]

    def body(*refs):
        step_kernel(begin, last, *factors, *refs)

    return pl.pallas_call(
        body,
        out_shape=tuple(out),
        in_specs=specs,
        out_specs=[VMEM] * len(out),
        scratch_shapes=scratch,
        compiler_params=PARAMS,
        cost_estimate=pl.CostEstimate(
            flops=10**11, bytes_accessed=10**9, transcendentals=0
        ),
        name="last_step" if last else "step",
    )(*args)


def final_kernel(own_ref, other_ref, sizes_ref, all_ref, blocks_ref, cols_ref, res_ref, res_out, norm_out, picked):
    amounts = take_amounts(own_ref, other_ref, all_ref, blocks_ref, picked)
    modes = amounts.shape[0] // 4
    half = res_ref.shape[1]
    high, low = split(amounts)
    total = jnp.zeros((1, 128), f32)
    for e in range(1, 3):
        at = slice(e * modes, (e + 2) * modes)
        spread = dot(cols_ref[e], jnp.concatenate([high[at], low[at]], axis=0))
        residual = res_ref[e - 1] + jnp.where(alive(sizes_ref[e], half), spread, 0.0)
        res_out[e - 1] = residual
        total += jnp.sum(residual * residual, axis=0, keepdims=True)
    norm_out[...] = total


def final(ints, sizes, everything, blocks, cols, residual):
    subs, _, width = blocks.shape
    lanes = residual.shape[-1]
    return pl.pallas_call(
        final_kernel,
        out_shape=(
            jax.ShapeDtypeStruct(residual.shape, f32),
            jax.ShapeDtypeStruct((1, lanes), f32),
        ),
        in_specs=[SMEM] * 3 + [VMEM] * 4,
        out_specs=[VMEM] * 2,
        scratch_shapes=[pltpu.VMEM((subs, 2 * width, lanes), bf16)],
        compiler_params=PARAMS,
        name="final",
    )(*ints, sizes, everything, blocks, cols, residual)


def trade(copies, axis):
    return lax.all_to_all(copies, axis, 0, 0, tiled=True)


def to_everyone(value, axis):
    size = lax.psum(1, axis)
    return trade(jnp.broadcast_to(value[None], (size, *value.shape)), axis)


def shards(dual_ops, modes, coarse_rows, coarse_cols, row_perm, iface_size, rhs):
    doms = lax.axis_size("dom")
    count, blocks, rows, _ = coarse_rows.shape
    flat = jnp.swapaxes(coarse_rows, 1, 2).reshape(count, rows, blocks * rows)
    whole = jnp.concatenate([coarse_cols, iface_size[:, None]], axis=1).astype(f32)
    whole = jnp.pad(whole, ((0, 0), (0, blocks * rows - whole.shape[1])))
    pack = jnp.concatenate([flat, jnp.broadcast_to(whole[:, None], (count, 8, blocks * rows))], axis=1)
    prior_pack = from_behind(pack[-1], "dom", 1)
    next_pack = from_behind(pack[0], "dom", -1)
    prior_rhs = from_behind(rhs[-1], "dom", 1)
    left, right, to_next, to_prior = slot_modes(modes, row_perm)
    prior_modes = from_behind(to_next, "dom", 1)
    next_modes = from_behind(to_prior, "dom", -1)
    ext = jnp.concatenate([prior_pack[None], pack, next_pack[None]], axis=0)
    ext_blocks = ext[:, :rows]
    ext_whole = ext[:, rows].astype(jnp.int32)
    cols = ext_whole[:, :blocks].reshape(-1)
    sizes = ext_whole[:3, blocks]
    odd = cols % 2
    own = 4 * (cols // 2) + 1 + odd
    other = (own + 4 * odd - 2) % (4 * doms)
    ints = (own, other)

    ops_a, diag_a = slot_op(dual_ops, row_perm[0:1], 0)
    row_forms, col_forms, part = start(sizes, left, right, prior_modes, next_modes, rhs)
    second_perm, _ = lax.optimization_barrier((row_perm[1:2], part))
    everything = trade(part, "dom").reshape(4 * doms, rows, -1)
    ops_b, diag_b = slot_op(dual_ops, second_perm, 1)
    ops = (ops_a, ops_b, diag_a, diag_b)

    centre = 0.5 * (high_bound + low_bound)
    radius = 0.5 * (high_bound - low_bound)
    spread_ratio = centre / radius
    ratios = [1.0 / spread_ratio]
    for _ in range(STEPS - 1):
        ratios.append(1.0 / (2.0 * spread_ratio - ratios[-1]))
    old = [0.0] + [ratios[t] * ratios[t - 1] for t in range(1, STEPS)]
    new = [1.0 / centre] + [2.0 * ratios[t] / radius for t in range(1, STEPS)]
    norms = []
    residual, direction, wa, wb, wc, sums, coarse_fields, links = first(
        new[0], sizes, rhs, prior_rhs, row_forms, col_forms, ops
    )
    solution = None
    for turn in range(STEPS):
        amounts, wa, wc, to_prior, to_next = coarse(
            new[turn], ints, everything, ext_blocks, wa, wc, coarse_fields
        )
        part = share(new[turn], amounts, sums, links)
        from_prior = from_behind(to_next, "dom", 1)
        from_next = from_behind(to_prior, "dom", -1)
        everything = trade(part, "dom").reshape(4 * doms, rows, -1)
        begin, last = turn == 0, turn + 1 == STEPS
        fields = (wa, wb, wc, from_prior, from_next, residual, direction)
        if not begin:
            fields += (solution,)
        if last:
            residual, solution, norm = step(
                begin, last, (new[turn], 0.0, 0.0), sizes, amounts, col_forms, coarse_fields, fields
            )
        else:
            factors = (new[turn], old[turn + 1], new[turn + 1])
            residual, solution, norm, direction, wa, wb, wc, sums = step(
                begin, last, factors, sizes, amounts, col_forms, coarse_fields, fields, row_forms, ops
            )
        if not begin:
            norms.append(norm)
    residual, norm = final(ints, sizes, everything, ext_blocks, col_forms, residual)
    norms.append(norm)
    sums = to_everyone(jnp.concatenate(norms, axis=0), ("dom", "case"))
    cases = lax.axis_size("case")
    totals = jnp.sum(sums.reshape(doms, cases, STEPS, -1), axis=0)
    whole_history = jnp.sqrt(totals + epsilon)
    history = lax.dynamic_index_in_dim(whole_history, lax.axis_index("case"), 0, keepdims=False)
    peak_norm = jnp.max(whole_history, axis=(0, 2))
    return (solution, residual, history, peak_norm)


def solution(mesh):
    in_specs = (
        P("dom", None, None),
        P("dom", None, None),
        P("dom", None, None, None),
        P("dom", None),
        P("dom", None),
        P("dom"),
        P("dom", None, "case"),
    )
    out_specs = (P("dom", None, "case"), P("dom", None, "case"), P(None, "case"), P())
    return jax.shard_map(shards, mesh=mesh, in_specs=in_specs, out_specs=out_specs, check_vma=False)
```

```python
import jax
import jax.numpy as jnp
from jax import lax
from jax.experimental import pallas as pl
from jax.experimental.pallas import tpu as pltpu
from jax.sharding import PartitionSpec as P

STEPS = 4

low_bound = 2.0
high_bound = 14.0
epsilon = 1e-06
f32 = jnp.float32
bf16 = jnp.bfloat16
BLK = 256
OPBLK = 512
VECBLK = 768
VMEM = pl.BlockSpec(memory_space=pltpu.VMEM)
SMEM = pl.BlockSpec(memory_space=pltpu.SMEM)
ANY = pl.BlockSpec(memory_space=pl.ANY)
PARAMS = pltpu.CompilerParams(vmem_limit_bytes=53000000)


def from_behind(block, axis, distance):
    count = lax.axis_size(axis)
    route = [((i - distance) % count, i) for i in range(count)]
    return lax.ppermute(block, axis, route)


def dot(a, b):
    return jnp.dot(a, b, preferred_element_type=f32)


def split(value):
    high = value.astype(bf16)
    low = (value - high.astype(f32)).astype(bf16)
    return high, low


def prepare_kernel(
    cols_ref, size_ref, modes_ref, perm_ref, coarse_ref, rhs_ref,
    left_ref, right_ref, own_ref, to_next_ref, to_prior_ref, rhs_rim, sem,
):
    count, rows, width = modes_ref.shape
    half = width // 2
    blocks = coarse_ref.shape[1]
    copy = pltpu.make_async_copy(rhs_ref.at[count - 1], rhs_rim, sem)
    copy.start()
    lane = lax.broadcasted_iota(jnp.int32, (8, 128), 1)
    for s in range(count):
        whole = jnp.zeros((8, 128), jnp.int32)
        for q in range(blocks):
            whole = jnp.where(lane == q, cols_ref[s, q], whole)
        whole = jnp.where(lane == blocks, size_ref[s], whole).astype(f32)
        flat = jnp.concatenate([coarse_ref[s, q] for q in range(blocks)], axis=1)
        both = jnp.concatenate([flat, whole], axis=0)
        own_ref[s] = both
        if s == 0:
            to_prior_ref[: rows + 8] = both
        if s == count - 1:
            to_next_ref[: rows + 8] = both
        for at in range(0, width, BLK):
            one_hot = (
                lax.broadcasted_iota(jnp.int32, (width, BLK), 0) == perm_ref[s : s + 1, at : at + BLK]
            ).astype(f32).astype(bf16)
            part = dot(modes_ref[s], one_hot)
            side, place = (left_ref, at) if at < half else (right_ref, at - half)
            side[s, :, place : place + BLK] = part.astype(bf16)
            rim = None
            if at < half and s == 0:
                rim = to_prior_ref
            if at >= half and s == count - 1:
                rim = to_next_ref
            if rim is not None:
                for k in range(0, BLK, 128):
                    row = rows + 8 + (place + k) // 128 * rows
                    rim[row : row + rows] = part[:, k : k + 128]
    copy.wait()


def prepare(coarse_cols, iface_size, modes, row_perm, coarse_rows, rhs):
    count, rows, width = modes.shape
    half = width // 2
    side = jax.ShapeDtypeStruct((count, rows, half), bf16)
    rim = jax.ShapeDtypeStruct((rows + 8 + half // 128 * rows, 128), f32)
    return pl.pallas_call(
        prepare_kernel,
        out_shape=(
            side,
            side,
            jax.ShapeDtypeStruct((count, rows + 8, 128), f32),
            rim,
            rim,
            jax.ShapeDtypeStruct(rhs.shape[1:], f32),
        ),
        in_specs=[SMEM, SMEM, VMEM, VMEM, VMEM, ANY],
        out_specs=[VMEM] * 5 + [ANY],
        scratch_shapes=[pltpu.SemaphoreType.DMA(())],
        compiler_params=PARAMS,
        name="prepare",
    )(coarse_cols, iface_size, modes, row_perm, coarse_rows, rhs)


def rim_modes(rim_ref, rows, half):
    first_row = rows + 8
    return jnp.concatenate(
        [rim_ref[first_row + k * rows : first_row + (k + 1) * rows] for k in range(half // 128)], axis=1
    )


def slot_op_kernel(ops_ref, perm_ref, out_ref, diag_ref, cols_done, one_hot, diag_row):
    width = one_hot.shape[0]
    blocks = width // OPBLK
    at = pl.program_id(0)

    @pl.when(at == 0)
    def _():
        for k in range(blocks):
            one_hot[k * OPBLK : (k + 1) * OPBLK, :] = (
                lax.broadcasted_iota(jnp.int32, (OPBLK, width), 0) + k * OPBLK == perm_ref[...]
            ).astype(f32).astype(bf16)
        diag_row[...] = jnp.zeros_like(diag_row)

    @pl.when(at < blocks)
    def _():
        block = ops_ref[0]
        on_diag = lax.broadcasted_iota(jnp.int32, (OPBLK, width), 0) + at * OPBLK == (
            lax.broadcasted_iota(jnp.int32, (OPBLK, width), 1)
        )
        diag_row[0:1, :] += jnp.sum(jnp.where(on_diag, block, 0.0), axis=0, keepdims=True)
        rest = jnp.where(on_diag, 0.0, block).astype(bf16)
        rows = pl.ds(pl.multiple_of(at * OPBLK, OPBLK), OPBLK)
        cols_done[rows, :] = dot(rest, one_hot[...]).astype(bf16)

    @pl.when(at >= blocks)
    def _():
        place = pl.multiple_of((at - blocks) * OPBLK, OPBLK)
        perm_part = perm_ref[:, pl.ds(place, OPBLK)].astype(f32)
        owner = jnp.transpose(jnp.broadcast_to(perm_part, (128, OPBLK)))
        total = jnp.zeros((OPBLK, 128), f32)
        pieces = []
        for k in range(0, width, 128):
            here = (lax.broadcasted_iota(jnp.int32, (OPBLK, 128), 1) + k).astype(f32) == owner
            pieces.append(here.astype(f32).astype(bf16))
            total += jnp.where(here, diag_row[0:1, k : k + 128], 0.0)
        out_ref[...] = dot(jnp.concatenate(pieces, axis=1), cols_done[...]).astype(bf16)
        diag_ref[...] = jnp.broadcast_to(jnp.sum(total, axis=1, keepdims=True), (OPBLK, 128))


def slot_op(dual_ops, perm_row, which):
    width = dual_ops.shape[1]
    blocks = width // OPBLK
    return pl.pallas_call(
        slot_op_kernel,
        grid=(2 * blocks,),
        out_shape=(
            jax.ShapeDtypeStruct((width, width), bf16),
            jax.ShapeDtypeStruct((width, 128), f32),
        ),
        in_specs=[
            pl.BlockSpec((1, OPBLK, width), lambda i: (which, jnp.minimum(i, blocks - 1), 0)),
            pl.BlockSpec((1, width), lambda i: (0, 0)),
        ],
        out_specs=[
            pl.BlockSpec((OPBLK, width), lambda i: (jnp.maximum(i - blocks, 0), 0)),
            pl.BlockSpec((OPBLK, 128), lambda i: (jnp.maximum(i - blocks, 0), 0)),
        ],
        scratch_shapes=[
            pltpu.VMEM((width, width), bf16),
            pltpu.VMEM((width, width), bf16),
            pltpu.VMEM((8, width), f32),
        ],
        compiler_params=PARAMS,
        cost_estimate=pl.CostEstimate(
            flops=4 * width**3, bytes_accessed=6 * width * width, transcendentals=0
        ),
        name="slot_op",
    )(dual_ops, perm_row)


def alive(size, rows):
    return lax.broadcasted_iota(jnp.int32, (rows, 128), 0) < size


def partial_coefficients(rows_ref, shares, part_ref):
    modes = part_ref.shape[2]
    sums = []
    for e, share in enumerate(shares):
        if share is None:
            sums.append(jnp.zeros((2 * modes, 128), f32))
            continue
        high, low = split(share)
        both = dot(rows_ref[e], jnp.concatenate([high, low], axis=1))
        sums.append(both[:, :128] + both[:, 128:])
    parts = [
        sums[0][:modes],
        sums[0][modes:] + sums[1][:modes],
        sums[1][modes:] + sums[2][:modes],
        sums[2][modes:],
    ]
    for k, part in enumerate(parts):
        part = part.astype(bf16)
        for device in range(part_ref.shape[0]):
            part_ref[device, k] = part


def start_kernel(
    count, ints_ref, left_ref, right_ref, prior_ref, next_ref, rhs_ref, rows_ref, cols_ref, part_ref
):
    half = rhs_ref.shape[1]
    modes = left_ref.shape[1]
    pairs = [
        (rim_modes(prior_ref, modes, half), left_ref[0]),
        (right_ref[0], left_ref[1]),
        (right_ref[1], rim_modes(next_ref, modes, half)),
    ]
    for e, (above, below) in enumerate(pairs):
        stack = jnp.concatenate([above.astype(f32), -below.astype(f32)], axis=0)
        rows_ref[e] = stack.astype(bf16)
        cols_ref[e] = jnp.transpose(jnp.concatenate([stack, stack], axis=0)).astype(bf16)
    shares = [None]
    for e in range(2):
        shares.append(jnp.where(alive(ints_ref[0, e + 1, count], half), -rhs_ref[e], 0.0))
    partial_coefficients(rows_ref, shares, part_ref)


def start(count, ints, left, right, prior, following, rhs):
    half = rhs.shape[1]
    modes = left.shape[1]

    def body(*refs):
        start_kernel(count, *refs)

    return pl.pallas_call(
        body,
        out_shape=(
            jax.ShapeDtypeStruct((3, 2 * modes, half), bf16),
            jax.ShapeDtypeStruct((3, half, 4 * modes), bf16),
            jax.ShapeDtypeStruct((lax.axis_size("dom"), 4, modes, 128), bf16),
        ),
        in_specs=[SMEM] + [VMEM] * 5,
        out_specs=[VMEM] * 3,
        compiler_params=PARAMS,
        name="start",
    )(ints, left, right, prior, following, rhs)


def triple(value):
    high, low = split(value)
    return jnp.concatenate([high, low, high, jnp.zeros_like(high)], axis=1)


def triple_rows(value):
    high, low = split(value)
    return jnp.concatenate([high, high, low, jnp.zeros_like(high)], axis=0)


def share_sums(rows_ref, shares):
    modes = rows_ref.shape[1] // 2
    sums = []
    for e, share in enumerate(shares):
        lanes = share.shape[1]
        high, low = split(share)
        both = dot(rows_ref[e], jnp.concatenate([high, low], axis=1))
        sums.append(both[:, :lanes] + both[:, lanes:])
    return jnp.concatenate(
        [
            sums[0][:modes],
            sums[0][modes:] + sums[1][:modes],
            sums[1][modes:] + sums[2][:modes],
            sums[2][modes:],
        ],
        axis=0,
    )


def own_shares(live, sides):
    return [
        jnp.where(live[0], -sides[0], 0.0),
        jnp.where(live[1], sides[1] - sides[2], 0.0),
        jnp.where(live[2], sides[3], 0.0),
    ]


def apply_operator(copies, held, slots, diag_refs, exact):
    sides = []
    half = exact(0).shape[0]
    for s in range(2):
        copies[s].wait()
        for side in range(2):
            here = slice(side * half, side * half + half)
            value = dot(held[s, here, :], slots[s])
            sign = 1.0 if side else -1.0
            lanes = exact(s + side).shape[1]
            diag = diag_refs[s][here, :]
            if lanes > 128:
                diag = jnp.concatenate([diag, diag], axis=1)
            sides.append(value + sign * (diag * exact(s + side)))
    return sides


def take_amounts(ints_ref, all_ref, packs, picked):
    prior_ref, own_ref, next_ref = packs
    modes = all_ref.shape[1]
    width = picked.shape[1] // 2
    count = width // modes
    blocks = [prior_ref[:modes], own_ref[0, :modes], own_ref[1, :modes], next_ref[:modes]]
    amounts = []
    for s, block in enumerate(blocks):
        for q in range(count):
            here = q * modes
            picked[s, here : here + modes, :] = all_ref[ints_ref[1, s, q]]
            picked[s, width + here : width + here + modes, :] = all_ref[ints_ref[2, s, q]]
        high, low = split(block)
        rows = jnp.concatenate([high, low], axis=0)
        both = dot(jnp.concatenate([rows, rows], axis=1), picked[s])
        amounts.append(both[:modes] + both[modes:])
    return jnp.concatenate(amounts, axis=0)


def first_kernel(
    scale, count, ints_ref, rhs_ref, prior_ref, rows_ref, cols_ref, op_a, op_b, diag_a, diag_b,
    res_out, dir_out, wa_out, wb_out, wc_out, sums_out, fields_out, links_out,
    held, slots, wide, sems,
):
    copies = []
    for s, op in enumerate((op_a, op_b)):
        copies.append(pltpu.make_async_copy(op, held.at[s], sems.at[s]))
        copies[-1].start()
    half = rhs_ref.shape[1]
    modes = rows_ref.shape[1] // 2
    live = [alive(ints_ref[0, e, count], half) for e in range(3)]
    for e in range(3):
        start = jnp.where(live[e], prior_ref[...] if e == 0 else rhs_ref[e - 1], 0.0)
        direction = scale * start
        res_out[e] = start
        dir_out[e] = direction
        pair = cols_ref[e][:, : 2 * modes].astype(f32)
        parts = [pair, jnp.zeros((half, 128 - 2 * modes), f32)]
        if e > 0:
            parts = [jnp.zeros((half, e * modes), f32), pair]
            parts.append(jnp.zeros((half, 128 - (2 + e) * modes), f32))
        coarse = jnp.where(live[e], jnp.concatenate(parts, axis=1), 0.0)
        both = jnp.concatenate([direction, coarse], axis=1)
        wide[e] = both
        low_form = both.astype(bf16)
        if e < 2:
            slots[e, :half] = -low_form
        if e > 0:
            slots[e - 1, half:] = low_form
    sides = apply_operator(copies, held, slots, (diag_a, diag_b), lambda e: wide[e])
    live = [jnp.concatenate([mask, mask], axis=1) for mask in live]
    shares = own_shares(live, sides)
    wa_out[...], wb_out[...], wc_out[...] = [share[:, :128] for share in shares]
    sums = share_sums(rows_ref, shares)
    sums_out[...] = sums[:, :128]
    for e in range(3):
        fields_out[e] = triple(shares[e][:, 128 : 128 + 4 * modes])
    links_out[...] = triple(sums[:, 128 : 128 + 4 * modes])


def scratch_of(half, lanes):
    return [
        pltpu.VMEM((2, 2 * half, 2 * half), bf16),
        pltpu.VMEM((2, 2 * half, lanes), bf16),
    ]


def first(scale, count, ints, rhs, prior_rhs, rows, cols, ops):
    half, lanes = rhs.shape[1:]
    modes = rows.shape[1] // 2
    field = jax.ShapeDtypeStruct((half, lanes), f32)
    three = jax.ShapeDtypeStruct((3, half, lanes), f32)

    def body(*refs):
        first_kernel(scale, count, *refs)

    return pl.pallas_call(
        body,
        out_shape=(
            three,
            three,
            field,
            field,
            field,
            jax.ShapeDtypeStruct((4 * modes, lanes), f32),
            jax.ShapeDtypeStruct((3, half, 16 * modes), bf16),
            jax.ShapeDtypeStruct((4 * modes, 16 * modes), bf16),
        ),
        in_specs=[SMEM] + [VMEM] * 4 + [ANY, ANY, VMEM, VMEM],
        out_specs=[VMEM] * 8,
        scratch_shapes=scratch_of(half, 2 * lanes)
        + [pltpu.VMEM((3, half, 2 * lanes), f32), pltpu.SemaphoreType.DMA((2,))],
        compiler_params=PARAMS,
        cost_estimate=pl.CostEstimate(
            flops=2 * 10**9, bytes_accessed=2 * 10**7, transcendentals=0
        ),
        name="first",
    )(ints, rhs, prior_rhs, rows, cols, *ops)


def coarse_kernel(
    new, ints_ref, all_ref, prior_ref, own_ref, next_ref,
    wa_ref, wc_ref, sums_ref, fields_ref, links_ref,
    amounts_out, wa_out, wc_out, to_prior_out, to_next_out, part_out, picked,
):
    amounts = take_amounts(ints_ref, all_ref, (prior_ref, own_ref, next_ref), picked)
    amounts_out[...] = amounts
    scaled = triple_rows(new * amounts)
    modes = part_out.shape[2]
    sums = (sums_ref[...] + dot(links_ref[...], scaled)).astype(bf16)
    for k in range(4):
        for device in range(part_out.shape[0]):
            part_out[device, k] = sums[k * modes : (k + 1) * modes]
    wa = wa_ref[...] + dot(fields_ref[0], scaled)
    wc = wc_ref[...] + dot(fields_ref[2], scaled)
    wa_out[...], wc_out[...] = wa, wc
    to_prior_out[...], to_next_out[...] = wa.astype(bf16), wc.astype(bf16)


def coarse(new, ints, everything, packs, wa, wc, sums, fields, links):
    modes = everything.shape[1]
    half, lanes = wa.shape
    subs, width = 4, packs[0].shape[1]
    field = jax.ShapeDtypeStruct((half, lanes), f32)
    rim = jax.ShapeDtypeStruct((half, lanes), bf16)

    def body(*refs):
        coarse_kernel(new, *refs)

    return pl.pallas_call(
        body,
        out_shape=(
            jax.ShapeDtypeStruct((4 * modes, lanes), f32),
            field,
            field,
            rim,
            rim,
            jax.ShapeDtypeStruct((everything.shape[0] // 4, 4, modes, lanes), bf16),
        ),
        in_specs=[SMEM] + [VMEM] * 9,
        out_specs=[VMEM] * 6,
        scratch_shapes=[pltpu.VMEM((subs, 2 * width, lanes), bf16)],
        compiler_params=PARAMS,
        cost_estimate=pl.CostEstimate(
            flops=10**8, bytes_accessed=4 * 10**6, transcendentals=0
        ),
        name="coarse",
    )(ints, everything, *packs, wa, wc, sums, fields, links)


def step_kernel(count, begin, last, new, old_next, new_next, *refs):
    refs = list(refs)
    take = lambda n: [refs.pop(0) for _ in range(n)]
    (ints_ref, amounts_ref, cols_ref, fields_ref) = take(4)
    wa_ref, wb_ref, wc_ref, prior_ref, next_ref, res_ref, dir_ref = take(7)
    sol_ref = None if begin else take(1)[0]
    if not last:
        rows_ref, op_a, op_b, diag_a, diag_b = take(5)
    res_out, sol_out, norm_out = take(3)
    if not last:
        dir_out, wa_out, wb_out, wc_out, sums_out = take(5)
        held, slots, sems = take(3)
        copies = []
        for s, op in enumerate((op_a, op_b)):
            copies.append(pltpu.make_async_copy(op, held.at[s], sems.at[s]))
            copies[-1].start()
    half = wa_ref.shape[0]
    modes = amounts_ref.shape[0] // 4
    amounts = amounts_ref[...]
    high, low = split(amounts)
    live = [alive(ints_ref[0, e, count], half) for e in range(3)]
    total = jnp.zeros((1, 128), f32)
    for e in range(3):
        if last and e == 0:
            continue
        at = slice(e * modes, (e + 2) * modes)
        spread = dot(cols_ref[e], jnp.concatenate([high[at], low[at]], axis=0))
        spread = jnp.where(live[e], spread, 0.0)
        if e == 0:
            field = wa_ref[...] + prior_ref[...].astype(f32)
        elif e == 1:
            field = wb_ref[...] + dot(fields_ref[1], triple_rows(new * amounts))
        else:
            field = wc_ref[...] + next_ref[...].astype(f32)
        residual = res_ref[e] + spread
        direction = dir_ref[e] + new * spread
        if e > 0:
            total += jnp.sum(residual * residual, axis=0, keepdims=True)
            sol_out[e - 1] = direction if begin else sol_ref[e - 1] + direction
        residual = residual - field
        if last:
            res_out[e - 1] = residual
            continue
        res_out[e] = residual
        direction = old_next * direction + new_next * residual
        dir_out[e] = direction
        low_form = direction.astype(bf16)
        if e < 2:
            slots[e, :half] = -low_form
        if e > 0:
            slots[e - 1, half:] = low_form
    norm_out[...] = total
    if last:
        return
    sides = apply_operator(copies, held, slots, (diag_a, diag_b), lambda e: dir_out[e])
    shares = own_shares(live, sides)
    wa_out[...], wb_out[...], wc_out[...] = shares
    sums_out[...] = share_sums(rows_ref, shares)


def step(count, begin, last, factors, ints, amounts, cols, coarse_fields, fields, rows=None, ops=()):
    half, lanes = fields[0].shape
    field = jax.ShapeDtypeStruct((half, lanes), f32)
    three = jax.ShapeDtypeStruct((3, half, lanes), f32)
    two = jax.ShapeDtypeStruct((2, half, lanes), f32)
    out = [two if last else three, two, jax.ShapeDtypeStruct((1, lanes), f32)]
    args = [ints, amounts, cols, coarse_fields, *fields]
    specs = [SMEM] + [VMEM] * (len(args) - 1)
    scratch = []
    if not last:
        out += [three, field, field, field, jax.ShapeDtypeStruct(amounts.shape, f32)]
        scratch += scratch_of(half, lanes) + [pltpu.SemaphoreType.DMA((2,))]
        args += [rows, *ops]
        specs += [VMEM, ANY, ANY, VMEM, VMEM]

    def body(*refs):
        step_kernel(count, begin, last, *factors, *refs)

    return pl.pallas_call(
        body,
        out_shape=tuple(out),
        in_specs=specs,
        out_specs=[VMEM] * len(out),
        scratch_shapes=scratch,
        compiler_params=PARAMS,
        cost_estimate=pl.CostEstimate(
            flops=10**11, bytes_accessed=10**9, transcendentals=0
        ),
        name="last_step" if last else "step",
    )(*args)


def final_kernel(
    count, ints_ref, all_ref, prior_ref, own_ref, next_ref, cols_ref, res_ref, norm_a, norm_b, norm_c,
    res_out, norm_out, picked,
):
    amounts = take_amounts(ints_ref, all_ref, (prior_ref, own_ref, next_ref), picked)
    modes = amounts.shape[0] // 4
    half = res_ref.shape[1]
    high, low = split(amounts)
    total = jnp.zeros((1, 128), f32)
    for e in range(1, 3):
        at = slice(e * modes, (e + 2) * modes)
        spread = dot(cols_ref[e], jnp.concatenate([high[at], low[at]], axis=0))
        residual = res_ref[e - 1] + jnp.where(alive(ints_ref[0, e, count], half), spread, 0.0)
        res_out[e - 1] = residual
        total += jnp.sum(residual * residual, axis=0, keepdims=True)
    norms = jnp.concatenate([norm_a[...], norm_b[...], norm_c[...], total], axis=0)
    for device in range(norm_out.shape[0]):
        norm_out[device] = norms


def final(count, ints, everything, packs, cols, residual, norms, devices):
    subs, width = 4, packs[0].shape[1]
    lanes = residual.shape[-1]

    def body(*refs):
        final_kernel(count, *refs)

    return pl.pallas_call(
        body,
        out_shape=(
            jax.ShapeDtypeStruct(residual.shape, f32),
            jax.ShapeDtypeStruct((devices, STEPS, lanes), f32),
        ),
        in_specs=[SMEM] + [VMEM] * 9,
        out_specs=[VMEM] * 2,
        scratch_shapes=[pltpu.VMEM((subs, 2 * width, lanes), bf16)],
        compiler_params=PARAMS,
        name="final",
    )(ints, everything, *packs, cols, residual, *norms)


def trade(copies, axis):
    return lax.all_to_all(copies, axis, 0, 0, tiled=True)


def shards(dual_ops, modes, coarse_rows, coarse_cols, row_perm, iface_size, rhs):
    doms = lax.axis_size("dom")
    count, blocks, rows, _ = coarse_rows.shape
    left, right, own_pack, to_next, to_prior, rhs_rim = prepare(
        coarse_cols, iface_size, modes, row_perm, coarse_rows, rhs
    )
    prior_pack = from_behind(to_next, "dom", 1)
    next_pack = from_behind(to_prior, "dom", -1)
    prior_rhs = from_behind(rhs_rim, "dom", 1)
    packs = (prior_pack, own_pack, next_pack)
    whole = jnp.concatenate(
        [prior_pack[rows : rows + 1], own_pack[:, rows], next_pack[rows : rows + 1]], axis=0
    ).astype(jnp.int32)
    odd = whole & 1
    own = 2 * (whole - odd) + 1 + odd
    other = own + 4 * odd - 2
    other = jnp.where(other < 0, other + 4 * doms, other)
    other = jnp.where(other >= 4 * doms, other - 4 * doms, other)
    ints = jnp.stack([whole, own, other])

    ops_a, diag_a = slot_op(dual_ops, row_perm[0:1], 0)
    row_forms, col_forms, part = start(blocks, ints, left, right, prior_pack, next_pack, rhs)
    second_perm, _ = lax.optimization_barrier((row_perm[1:2], part))
    everything = trade(part, "dom").reshape(4 * doms, rows, -1)
    ops_b, diag_b = slot_op(dual_ops, second_perm, 1)
    ops = (ops_a, ops_b, diag_a, diag_b)

    centre = 0.5 * (high_bound + low_bound)
    radius = 0.5 * (high_bound - low_bound)
    spread_ratio = centre / radius
    ratios = [1.0 / spread_ratio]
    for _ in range(STEPS - 1):
        ratios.append(1.0 / (2.0 * spread_ratio - ratios[-1]))
    old = [0.0] + [ratios[t] * ratios[t - 1] for t in range(1, STEPS)]
    new = [1.0 / centre] + [2.0 * ratios[t] / radius for t in range(1, STEPS)]
    norms = []
    residual, direction, wa, wb, wc, sums, coarse_fields, links = first(
        new[0], blocks, ints, rhs, prior_rhs, row_forms, col_forms, ops
    )
    solution = None
    for turn in range(STEPS):
        amounts, wa, wc, to_prior, to_next, part = coarse(
            new[turn], ints, everything, packs, wa, wc, sums, coarse_fields, links
        )
        from_prior = from_behind(to_next, "dom", 1)
        from_next = from_behind(to_prior, "dom", -1)
        everything = trade(part, "dom").reshape(4 * doms, rows, -1)
        begin, last = turn == 0, turn + 1 == STEPS
        fields = (wa, wb, wc, from_prior, from_next, residual, direction)
        if not begin:
            fields += (solution,)
        if last:
            residual, solution, norm = step(
                blocks, begin, last, (new[turn], 0.0, 0.0), ints, amounts, col_forms, coarse_fields, fields
            )
        else:
            factors = (new[turn], old[turn + 1], new[turn + 1])
            residual, solution, norm, direction, wa, wb, wc, sums = step(
                blocks, begin, last, factors, ints, amounts, col_forms, coarse_fields, fields, row_forms, ops
            )
        if not begin:
            norms.append(norm)
    cases = lax.axis_size("case")
    residual, sums = final(
        blocks, ints, everything, packs, col_forms, residual, norms, doms * cases
    )
    sums = trade(sums, ("dom", "case"))
    totals = jnp.sum(sums.reshape(doms, cases, STEPS, -1), axis=0)
    whole_history = jnp.sqrt(totals + epsilon)
    history = lax.dynamic_index_in_dim(whole_history, lax.axis_index("case"), 0, keepdims=False)
    peak_norm = jnp.max(whole_history, axis=(0, 2))
    return (solution, residual, history, peak_norm)


def solution(mesh):
    in_specs = (
        P("dom", None, None),
        P("dom", None, None),
        P("dom", None, None, None),
        P("dom", None),
        P("dom", None),
        P("dom"),
        P("dom", None, "case"),
    )
    out_specs = (P("dom", None, "case"), P("dom", None, "case"), P(None, "case"), P())
    return jax.shard_map(shards, mesh=mesh, in_specs=in_specs, out_specs=out_specs, check_vma=False)
```

```python
import jax
import jax.numpy as jnp
from jax import lax
from jax.experimental import pallas as pl
from jax.experimental.pallas import tpu as pltpu
from jax.sharding import PartitionSpec as P

STEPS = 4

low_bound = 2.0
high_bound = 14.0
epsilon = 1e-06
f32 = jnp.float32
bf16 = jnp.bfloat16
BLK = 256
OPBLK = 512
VECBLK = 768
VMEM = pl.BlockSpec(memory_space=pltpu.VMEM)
SMEM = pl.BlockSpec(memory_space=pltpu.SMEM)
ANY = pl.BlockSpec(memory_space=pl.ANY)
WHOLE = pltpu.CompilerParams(vmem_limit_bytes=60 * 1024 * 1024)
PARAMS = pltpu.CompilerParams(vmem_limit_bytes=53000000)


def from_behind(block, axis, distance):
    count = lax.axis_size(axis)
    route = [((i - distance) % count, i) for i in range(count)]
    return lax.ppermute(block, axis, route)


def dot(a, b):
    return jnp.dot(a, b, preferred_element_type=f32)


def split(value):
    high = value.astype(bf16)
    low = (value - high.astype(f32)).astype(bf16)
    return high, low


def prepare_kernel(
    cols_ref, size_ref, modes_ref, perm_ref, coarse_ref, rhs_ref,
    left_ref, right_ref, own_ref, to_next_ref, to_prior_ref, rhs_rim, sem,
):
    count, rows, width = modes_ref.shape
    half = width // 2
    blocks = coarse_ref.shape[1]
    copy = pltpu.make_async_copy(rhs_ref.at[count - 1], rhs_rim, sem)
    copy.start()
    lane = lax.broadcasted_iota(jnp.int32, (8, 128), 1)
    for s in range(count):
        whole = jnp.zeros((8, 128), jnp.int32)
        for q in range(blocks):
            whole = jnp.where(lane == q, cols_ref[s, q], whole)
        whole = jnp.where(lane == blocks, size_ref[s], whole).astype(f32)
        flat = jnp.concatenate([coarse_ref[s, q] for q in range(blocks)], axis=1)
        both = jnp.concatenate([flat, whole], axis=0)
        own_ref[s] = both
        if s == 0:
            to_prior_ref[: rows + 8] = both
        if s == count - 1:
            to_next_ref[: rows + 8] = both
        for at in range(0, width, BLK):
            one_hot = (
                lax.broadcasted_iota(jnp.int32, (width, BLK), 0) == perm_ref[s : s + 1, at : at + BLK]
            ).astype(f32).astype(bf16)
            part = dot(modes_ref[s], one_hot)
            side, place = (left_ref, at) if at < half else (right_ref, at - half)
            side[s, :, place : place + BLK] = part.astype(bf16)
            rim = None
            if at < half and s == 0:
                rim = to_prior_ref
            if at >= half and s == count - 1:
                rim = to_next_ref
            if rim is not None:
                for k in range(0, BLK, 128):
                    row = rows + 8 + (place + k) // 128 * rows
                    rim[row : row + rows] = part[:, k : k + 128]
    copy.wait()


def prepare(coarse_cols, iface_size, modes, row_perm, coarse_rows, rhs):
    count, rows, width = modes.shape
    half = width // 2
    side = jax.ShapeDtypeStruct((count, rows, half), bf16)
    rim = jax.ShapeDtypeStruct((rows + 8 + half // 128 * rows, 128), f32)
    return pl.pallas_call(
        prepare_kernel,
        out_shape=(
            side,
            side,
            jax.ShapeDtypeStruct((count, rows + 8, 128), f32),
            rim,
            rim,
            jax.ShapeDtypeStruct(rhs.shape[1:], f32),
        ),
        in_specs=[SMEM, SMEM, VMEM, VMEM, VMEM, ANY],
        out_specs=[VMEM] * 6,
        scratch_shapes=[pltpu.SemaphoreType.DMA(())],
        compiler_params=WHOLE,
        name="prepare",
    )(coarse_cols, iface_size, modes, row_perm, coarse_rows, rhs)


def rim_modes(rim_ref, rows, half):
    first_row = rows + 8
    return jnp.concatenate(
        [rim_ref[first_row + k * rows : first_row + (k + 1) * rows] for k in range(half // 128)], axis=1
    )


def slot_op_kernel(ops_ref, perm_ref, out_ref, diag_ref, cols_done, one_hot, diag_row):
    width = one_hot.shape[0]
    blocks = width // OPBLK
    at = pl.program_id(0)

    @pl.when(at == 0)
    def _():
        for k in range(blocks):
            one_hot[k * OPBLK : (k + 1) * OPBLK, :] = (
                lax.broadcasted_iota(jnp.int32, (OPBLK, width), 0) + k * OPBLK == perm_ref[...]
            ).astype(f32).astype(bf16)
        diag_row[...] = jnp.zeros_like(diag_row)

    @pl.when(at < blocks)
    def _():
        block = ops_ref[0]
        on_diag = lax.broadcasted_iota(jnp.int32, (OPBLK, width), 0) + at * OPBLK == (
            lax.broadcasted_iota(jnp.int32, (OPBLK, width), 1)
        )
        diag_row[0:1, :] += jnp.sum(jnp.where(on_diag, block, 0.0), axis=0, keepdims=True)
        rest = jnp.where(on_diag, 0.0, block).astype(bf16)
        rows = pl.ds(pl.multiple_of(at * OPBLK, OPBLK), OPBLK)
        cols_done[rows, :] = dot(rest, one_hot[...]).astype(bf16)

    @pl.when(at >= blocks)
    def _():
        place = pl.multiple_of((at - blocks) * OPBLK, OPBLK)
        perm_part = perm_ref[:, pl.ds(place, OPBLK)].astype(f32)
        owner = jnp.transpose(jnp.broadcast_to(perm_part, (128, OPBLK)))
        total = jnp.zeros((OPBLK, 128), f32)
        pieces = []
        for k in range(0, width, 128):
            here = (lax.broadcasted_iota(jnp.int32, (OPBLK, 128), 1) + k).astype(f32) == owner
            pieces.append(here.astype(f32).astype(bf16))
            total += jnp.where(here, diag_row[0:1, k : k + 128], 0.0)
        out_ref[...] = dot(jnp.concatenate(pieces, axis=1), cols_done[...]).astype(bf16)
        diag_ref[...] = jnp.broadcast_to(jnp.sum(total, axis=1, keepdims=True), (OPBLK, 128))


def slot_op(dual_ops, perm_row, which):
    width = dual_ops.shape[1]
    blocks = width // OPBLK
    return pl.pallas_call(
        slot_op_kernel,
        grid=(2 * blocks,),
        out_shape=(
            jax.ShapeDtypeStruct((width, width), bf16),
            jax.ShapeDtypeStruct((width, 128), f32),
        ),
        in_specs=[
            pl.BlockSpec((1, OPBLK, width), lambda i: (which, jnp.minimum(i, blocks - 1), 0)),
            pl.BlockSpec((1, width), lambda i: (0, 0)),
        ],
        out_specs=[
            pl.BlockSpec((OPBLK, width), lambda i: (jnp.maximum(i - blocks, 0), 0)),
            pl.BlockSpec((OPBLK, 128), lambda i: (jnp.maximum(i - blocks, 0), 0)),
        ],
        scratch_shapes=[
            pltpu.VMEM((width, width), bf16),
            pltpu.VMEM((width, width), bf16),
            pltpu.VMEM((8, width), f32),
        ],
        compiler_params=PARAMS,
        cost_estimate=pl.CostEstimate(
            flops=4 * width**3, bytes_accessed=6 * width * width, transcendentals=0
        ),
        name="slot_op",
    )(dual_ops, perm_row)


def alive(size, rows):
    return lax.broadcasted_iota(jnp.int32, (rows, 128), 0) < size


def partial_coefficients(rows_ref, shares, part_ref):
    modes = part_ref.shape[2]
    sums = []
    for e, share in enumerate(shares):
        if share is None:
            sums.append(jnp.zeros((2 * modes, 128), f32))
            continue
        high, low = split(share)
        both = dot(rows_ref[e], jnp.concatenate([high, low], axis=1))
        sums.append(both[:, :128] + both[:, 128:])
    parts = [
        sums[0][:modes],
        sums[0][modes:] + sums[1][:modes],
        sums[1][modes:] + sums[2][:modes],
        sums[2][modes:],
    ]
    for k, part in enumerate(parts):
        part = part.astype(bf16)
        for device in range(part_ref.shape[0]):
            part_ref[device, k] = part


def start_kernel(
    count, ints_ref, left_ref, right_ref, prior_ref, next_ref, rhs_ref, rows_ref, cols_ref, part_ref
):
    half = rhs_ref.shape[1]
    modes = left_ref.shape[1]
    pairs = [
        (rim_modes(prior_ref, modes, half), left_ref[0]),
        (right_ref[0], left_ref[1]),
        (right_ref[1], rim_modes(next_ref, modes, half)),
    ]
    for e, (above, below) in enumerate(pairs):
        stack = jnp.concatenate([above.astype(f32), -below.astype(f32)], axis=0)
        rows_ref[e] = stack.astype(bf16)
        cols_ref[e] = jnp.transpose(jnp.concatenate([stack, stack], axis=0)).astype(bf16)
    shares = [None]
    for e in range(2):
        shares.append(jnp.where(alive(ints_ref[0, e + 1, count], half), -rhs_ref[e], 0.0))
    partial_coefficients(rows_ref, shares, part_ref)


def start(count, ints, left, right, prior, following, rhs):
    half = rhs.shape[1]
    modes = left.shape[1]

    def body(*refs):
        start_kernel(count, *refs)

    return pl.pallas_call(
        body,
        out_shape=(
            jax.ShapeDtypeStruct((3, 2 * modes, half), bf16),
            jax.ShapeDtypeStruct((3, half, 4 * modes), bf16),
            jax.ShapeDtypeStruct((lax.axis_size("dom"), 4, modes, 128), bf16),
        ),
        in_specs=[SMEM] + [VMEM] * 5,
        out_specs=[VMEM] * 3,
        compiler_params=PARAMS,
        name="start",
    )(ints, left, right, prior, following, rhs)


def triple(value):
    high, low = split(value)
    return jnp.concatenate([high, low, high, jnp.zeros_like(high)], axis=1)


def triple_rows(value):
    high, low = split(value)
    return jnp.concatenate([high, high, low, jnp.zeros_like(high)], axis=0)


def share_sums(rows_ref, shares):
    modes = rows_ref.shape[1] // 2
    sums = []
    for e, share in enumerate(shares):
        lanes = share.shape[1]
        high, low = split(share)
        both = dot(rows_ref[e], jnp.concatenate([high, low], axis=1))
        sums.append(both[:, :lanes] + both[:, lanes:])
    return jnp.concatenate(
        [
            sums[0][:modes],
            sums[0][modes:] + sums[1][:modes],
            sums[1][modes:] + sums[2][:modes],
            sums[2][modes:],
        ],
        axis=0,
    )


def own_shares(live, sides):
    return [
        jnp.where(live[0], -sides[0], 0.0),
        jnp.where(live[1], sides[1] - sides[2], 0.0),
        jnp.where(live[2], sides[3], 0.0),
    ]


def apply_operator(copies, held, slots, diag_refs, exact):
    sides = []
    half = exact(0).shape[0]
    for s in range(2):
        copies[s].wait()
        for side in range(2):
            here = slice(side * half, side * half + half)
            value = dot(held[s, here, :], slots[s])
            sign = 1.0 if side else -1.0
            lanes = exact(s + side).shape[1]
            diag = diag_refs[s][here, :]
            if lanes > 128:
                diag = jnp.concatenate([diag, diag], axis=1)
            sides.append(value + sign * (diag * exact(s + side)))
    return sides


def take_amounts(ints_ref, all_ref, packs, picked):
    prior_ref, own_ref, next_ref = packs
    modes = all_ref.shape[1]
    width = picked.shape[1] // 2
    count = width // modes
    blocks = [prior_ref[:modes], own_ref[0, :modes], own_ref[1, :modes], next_ref[:modes]]
    amounts = []
    for s, block in enumerate(blocks):
        for q in range(count):
            here = q * modes
            picked[s, here : here + modes, :] = all_ref[ints_ref[1, s, q]]
            picked[s, width + here : width + here + modes, :] = all_ref[ints_ref[2, s, q]]
        high, low = split(block)
        rows = jnp.concatenate([high, low], axis=0)
        both = dot(jnp.concatenate([rows, rows], axis=1), picked[s])
        amounts.append(both[:modes] + both[modes:])
    return jnp.concatenate(amounts, axis=0)


def first_kernel(
    scale, count, ints_ref, rhs_ref, prior_ref, rows_ref, cols_ref, op_a, op_b, diag_a, diag_b,
    res_out, dir_out, wa_out, wb_out, wc_out, sums_out, fields_out, links_out,
    held, slots, wide, sems,
):
    copies = []
    for s, op in enumerate((op_a, op_b)):
        copies.append(pltpu.make_async_copy(op, held.at[s], sems.at[s]))
        copies[-1].start()
    half = rhs_ref.shape[1]
    modes = rows_ref.shape[1] // 2
    live = [alive(ints_ref[0, e, count], half) for e in range(3)]
    for e in range(3):
        start = jnp.where(live[e], prior_ref[...] if e == 0 else rhs_ref[e - 1], 0.0)
        direction = scale * start
        res_out[e] = start
        dir_out[e] = direction
        pair = cols_ref[e][:, : 2 * modes].astype(f32)
        parts = [pair, jnp.zeros((half, 128 - 2 * modes), f32)]
        if e > 0:
            parts = [jnp.zeros((half, e * modes), f32), pair]
            parts.append(jnp.zeros((half, 128 - (2 + e) * modes), f32))
        coarse = jnp.where(live[e], jnp.concatenate(parts, axis=1), 0.0)
        both = jnp.concatenate([direction, coarse], axis=1)
        wide[e] = both
        low_form = both.astype(bf16)
        if e < 2:
            slots[e, :half] = -low_form
        if e > 0:
            slots[e - 1, half:] = low_form
    sides = apply_operator(copies, held, slots, (diag_a, diag_b), lambda e: wide[e])
    live = [jnp.concatenate([mask, mask], axis=1) for mask in live]
    shares = own_shares(live, sides)
    wa_out[...], wb_out[...], wc_out[...] = [share[:, :128] for share in shares]
    sums = share_sums(rows_ref, shares)
    sums_out[...] = sums[:, :128]
    for e in range(3):
        fields_out[e] = triple(shares[e][:, 128 : 128 + 4 * modes])
    links_out[...] = triple(sums[:, 128 : 128 + 4 * modes])


def scratch_of(half, lanes):
    return [
        pltpu.VMEM((2, 2 * half, 2 * half), bf16),
        pltpu.VMEM((2, 2 * half, lanes), bf16),
    ]


def first(scale, count, ints, rhs, prior_rhs, rows, cols, ops):
    half, lanes = rhs.shape[1:]
    modes = rows.shape[1] // 2
    field = jax.ShapeDtypeStruct((half, lanes), f32)
    three = jax.ShapeDtypeStruct((3, half, lanes), f32)

    def body(*refs):
        first_kernel(scale, count, *refs)

    return pl.pallas_call(
        body,
        out_shape=(
            three,
            three,
            field,
            field,
            field,
            jax.ShapeDtypeStruct((4 * modes, lanes), f32),
            jax.ShapeDtypeStruct((3, half, 16 * modes), bf16),
            jax.ShapeDtypeStruct((4 * modes, 16 * modes), bf16),
        ),
        in_specs=[SMEM] + [VMEM] * 4 + [ANY, ANY, VMEM, VMEM],
        out_specs=[VMEM] * 8,
        scratch_shapes=scratch_of(half, 2 * lanes)
        + [pltpu.VMEM((3, half, 2 * lanes), f32), pltpu.SemaphoreType.DMA((2,))],
        compiler_params=PARAMS,
        cost_estimate=pl.CostEstimate(
            flops=2 * 10**9, bytes_accessed=2 * 10**7, transcendentals=0
        ),
        name="first",
    )(ints, rhs, prior_rhs, rows, cols, *ops)


def coarse_kernel(
    new, ints_ref, all_ref, prior_ref, own_ref, next_ref,
    wa_ref, wc_ref, sums_ref, fields_ref, links_ref,
    amounts_out, wa_out, wc_out, to_prior_out, to_next_out, part_out, picked,
):
    amounts = take_amounts(ints_ref, all_ref, (prior_ref, own_ref, next_ref), picked)
    amounts_out[...] = amounts
    scaled = triple_rows(new * amounts)
    modes = part_out.shape[2]
    sums = (sums_ref[...] + dot(links_ref[...], scaled)).astype(bf16)
    for k in range(4):
        for device in range(part_out.shape[0]):
            part_out[device, k] = sums[k * modes : (k + 1) * modes]
    wa = wa_ref[...] + dot(fields_ref[0], scaled)
    wc = wc_ref[...] + dot(fields_ref[2], scaled)
    wa_out[...], wc_out[...] = wa, wc
    to_prior_out[...], to_next_out[...] = wa.astype(bf16), wc.astype(bf16)


def coarse(new, ints, everything, packs, wa, wc, sums, fields, links):
    modes = everything.shape[1]
    half, lanes = wa.shape
    subs, width = 4, packs[0].shape[1]
    field = jax.ShapeDtypeStruct((half, lanes), f32)
    rim = jax.ShapeDtypeStruct((half, lanes), bf16)

    def body(*refs):
        coarse_kernel(new, *refs)

    return pl.pallas_call(
        body,
        out_shape=(
            jax.ShapeDtypeStruct((4 * modes, lanes), f32),
            field,
            field,
            rim,
            rim,
            jax.ShapeDtypeStruct((everything.shape[0] // 4, 4, modes, lanes), bf16),
        ),
        in_specs=[SMEM] + [VMEM] * 9,
        out_specs=[VMEM] * 6,
        scratch_shapes=[pltpu.VMEM((subs, 2 * width, lanes), bf16)],
        compiler_params=PARAMS,
        cost_estimate=pl.CostEstimate(
            flops=10**8, bytes_accessed=4 * 10**6, transcendentals=0
        ),
        name="coarse",
    )(ints, everything, *packs, wa, wc, sums, fields, links)


def step_kernel(count, begin, last, new, old_next, new_next, *refs):
    refs = list(refs)
    take = lambda n: [refs.pop(0) for _ in range(n)]
    (ints_ref, amounts_ref, cols_ref, fields_ref) = take(4)
    wa_ref, wb_ref, wc_ref, prior_ref, next_ref, res_ref, dir_ref = take(7)
    sol_ref = None if begin else take(1)[0]
    if not last:
        rows_ref, op_a, op_b, diag_a, diag_b = take(5)
    res_out, sol_out, norm_out = take(3)
    if not last:
        dir_out, wa_out, wb_out, wc_out, sums_out = take(5)
        held, slots, sems = take(3)
        copies = []
        for s, op in enumerate((op_a, op_b)):
            copies.append(pltpu.make_async_copy(op, held.at[s], sems.at[s]))
            copies[-1].start()
    half = wa_ref.shape[0]
    modes = amounts_ref.shape[0] // 4
    amounts = amounts_ref[...]
    high, low = split(amounts)
    live = [alive(ints_ref[0, e, count], half) for e in range(3)]
    total = jnp.zeros((1, 128), f32)
    for e in range(3):
        if last and e == 0:
            continue
        at = slice(e * modes, (e + 2) * modes)
        spread = dot(cols_ref[e], jnp.concatenate([high[at], low[at]], axis=0))
        spread = jnp.where(live[e], spread, 0.0)
        if e == 0:
            field = wa_ref[...] + prior_ref[...].astype(f32)
        elif e == 1:
            field = wb_ref[...] + dot(fields_ref[1], triple_rows(new * amounts))
        else:
            field = wc_ref[...] + next_ref[...].astype(f32)
        residual = res_ref[e] + spread
        direction = dir_ref[e] + new * spread
        if e > 0:
            total += jnp.sum(residual * residual, axis=0, keepdims=True)
            sol_out[e - 1] = direction if begin else sol_ref[e - 1] + direction
        residual = residual - field
        if last:
            res_out[e - 1] = residual
            continue
        res_out[e] = residual
        direction = old_next * direction + new_next * residual
        dir_out[e] = direction
        low_form = direction.astype(bf16)
        if e < 2:
            slots[e, :half] = -low_form
        if e > 0:
            slots[e - 1, half:] = low_form
    norm_out[...] = total
    if last:
        return
    sides = apply_operator(copies, held, slots, (diag_a, diag_b), lambda e: dir_out[e])
    shares = own_shares(live, sides)
    wa_out[...], wb_out[...], wc_out[...] = shares
    sums_out[...] = share_sums(rows_ref, shares)


def step(count, begin, last, factors, ints, amounts, cols, coarse_fields, fields, rows=None, ops=()):
    half, lanes = fields[0].shape
    field = jax.ShapeDtypeStruct((half, lanes), f32)
    three = jax.ShapeDtypeStruct((3, half, lanes), f32)
    two = jax.ShapeDtypeStruct((2, half, lanes), f32)
    out = [two if last else three, two, jax.ShapeDtypeStruct((1, lanes), f32)]
    args = [ints, amounts, cols, coarse_fields, *fields]
    specs = [SMEM] + [VMEM] * (len(args) - 1)
    scratch = []
    if not last:
        out += [three, field, field, field, jax.ShapeDtypeStruct(amounts.shape, f32)]
        scratch += scratch_of(half, lanes) + [pltpu.SemaphoreType.DMA((2,))]
        args += [rows, *ops]
        specs += [VMEM, ANY, ANY, VMEM, VMEM]

    def body(*refs):
        step_kernel(count, begin, last, *factors, *refs)

    return pl.pallas_call(
        body,
        out_shape=tuple(out),
        in_specs=specs,
        out_specs=[VMEM] * len(out),
        scratch_shapes=scratch,
        compiler_params=PARAMS,
        cost_estimate=pl.CostEstimate(
            flops=10**11, bytes_accessed=10**9, transcendentals=0
        ),
        name="last_step" if last else "step",
    )(*args)


def final_kernel(
    count, ints_ref, all_ref, prior_ref, own_ref, next_ref, cols_ref, res_ref, norm_a, norm_b, norm_c,
    res_out, norm_out, picked,
):
    amounts = take_amounts(ints_ref, all_ref, (prior_ref, own_ref, next_ref), picked)
    modes = amounts.shape[0] // 4
    half = res_ref.shape[1]
    high, low = split(amounts)
    total = jnp.zeros((1, 128), f32)
    for e in range(1, 3):
        at = slice(e * modes, (e + 2) * modes)
        spread = dot(cols_ref[e], jnp.concatenate([high[at], low[at]], axis=0))
        residual = res_ref[e - 1] + jnp.where(alive(ints_ref[0, e, count], half), spread, 0.0)
        res_out[e - 1] = residual
        total += jnp.sum(residual * residual, axis=0, keepdims=True)
    norms = jnp.concatenate([norm_a[...], norm_b[...], norm_c[...], total], axis=0)
    for device in range(norm_out.shape[0]):
        norm_out[device] = norms


def final(count, ints, everything, packs, cols, residual, norms, devices):
    subs, width = 4, packs[0].shape[1]
    lanes = residual.shape[-1]

    def body(*refs):
        final_kernel(count, *refs)

    return pl.pallas_call(
        body,
        out_shape=(
            jax.ShapeDtypeStruct(residual.shape, f32),
            jax.ShapeDtypeStruct((devices, STEPS, lanes), f32),
        ),
        in_specs=[SMEM] + [VMEM] * 9,
        out_specs=[VMEM] * 2,
        scratch_shapes=[pltpu.VMEM((subs, 2 * width, lanes), bf16)],
        compiler_params=PARAMS,
        name="final",
    )(ints, everything, *packs, cols, residual, *norms)


def trade(copies, axis):
    return lax.all_to_all(copies, axis, 0, 0, tiled=True)


def shards(dual_ops, modes, coarse_rows, coarse_cols, row_perm, iface_size, rhs):
    doms = lax.axis_size("dom")
    count, blocks, rows, _ = coarse_rows.shape
    left, right, own_pack, to_next, to_prior, rhs_rim = prepare(
        coarse_cols, iface_size, modes, row_perm, coarse_rows, rhs
    )
    prior_pack = from_behind(to_next, "dom", 1)
    next_pack = from_behind(to_prior, "dom", -1)
    prior_rhs = from_behind(rhs_rim, "dom", 1)
    packs = (prior_pack, own_pack, next_pack)
    whole = jnp.concatenate(
        [prior_pack[rows : rows + 1], own_pack[:, rows], next_pack[rows : rows + 1]], axis=0
    ).astype(jnp.int32)
    odd = whole & 1
    own = 2 * (whole - odd) + 1 + odd
    other = own + 4 * odd - 2
    other = jnp.where(other < 0, other + 4 * doms, other)
    other = jnp.where(other >= 4 * doms, other - 4 * doms, other)
    ints = jnp.stack([whole, own, other])

    ops_a, diag_a = slot_op(dual_ops, row_perm[0:1], 0)
    row_forms, col_forms, part = start(blocks, ints, left, right, prior_pack, next_pack, rhs)
    second_perm, _ = lax.optimization_barrier((row_perm[1:2], part))
    everything = trade(part, "dom").reshape(4 * doms, rows, -1)
    ops_b, diag_b = slot_op(dual_ops, second_perm, 1)
    ops = (ops_a, ops_b, diag_a, diag_b)

    centre = 0.5 * (high_bound + low_bound)
    radius = 0.5 * (high_bound - low_bound)
    spread_ratio = centre / radius
    ratios = [1.0 / spread_ratio]
    for _ in range(STEPS - 1):
        ratios.append(1.0 / (2.0 * spread_ratio - ratios[-1]))
    old = [0.0] + [ratios[t] * ratios[t - 1] for t in range(1, STEPS)]
    new = [1.0 / centre] + [2.0 * ratios[t] / radius for t in range(1, STEPS)]
    norms = []
    residual, direction, wa, wb, wc, sums, coarse_fields, links = first(
        new[0], blocks, ints, rhs, prior_rhs, row_forms, col_forms, ops
    )
    solution = None
    for turn in range(STEPS):
        amounts, wa, wc, to_prior, to_next, part = coarse(
            new[turn], ints, everything, packs, wa, wc, sums, coarse_fields, links
        )
        from_prior = from_behind(to_next, "dom", 1)
        from_next = from_behind(to_prior, "dom", -1)
        everything = trade(part, "dom").reshape(4 * doms, rows, -1)
        begin, last = turn == 0, turn + 1 == STEPS
        fields = (wa, wb, wc, from_prior, from_next, residual, direction)
        if not begin:
            fields += (solution,)
        if last:
            residual, solution, norm = step(
                blocks, begin, last, (new[turn], 0.0, 0.0), ints, amounts, col_forms, coarse_fields, fields
            )
        else:
            factors = (new[turn], old[turn + 1], new[turn + 1])
            residual, solution, norm, direction, wa, wb, wc, sums = step(
                blocks, begin, last, factors, ints, amounts, col_forms, coarse_fields, fields, row_forms, ops
            )
        if not begin:
            norms.append(norm)
    cases = lax.axis_size("case")
    residual, sums = final(
        blocks, ints, everything, packs, col_forms, residual, norms, doms * cases
    )
    sums = trade(sums, ("dom", "case"))
    totals = jnp.sum(sums.reshape(doms, cases, STEPS, -1), axis=0)
    whole_history = jnp.sqrt(totals + epsilon)
    history = lax.dynamic_index_in_dim(whole_history, lax.axis_index("case"), 0, keepdims=False)
    peak_norm = jnp.max(whole_history, axis=(0, 2))
    return (solution, residual, history, peak_norm)


def solution(mesh):
    in_specs = (
        P("dom", None, None),
        P("dom", None, None),
        P("dom", None, None, None),
        P("dom", None),
        P("dom", None),
        P("dom"),
        P("dom", None, "case"),
    )
    out_specs = (P("dom", None, "case"), P("dom", None, "case"), P(None, "case"), P())
    return jax.shard_map(shards, mesh=mesh, in_specs=in_specs, out_specs=out_specs, check_vma=False)
```
